32 devices in a mesh: dp: 4 (over z), seq: 4 (over y, x), mp: 2 (over core).
Axes of the slice: x: 2, y: 2, z: 4, core: 2. Of those that a mesh axis runs over, the one named last changes fastest.
Arguments:
- inputs: float32 [4, 512, 768], P('dp', 'seq'), may hold values from -6 to 6
- span_info: int32 [4, 16, 2], P('dp', 'seq'), may hold values from 1 to 510, as said below
- mask_vector: float32 [768], replicated, may hold values from -5 to 5
- w_query: bfloat16 [2, 768, 768], P(None, None, 'mp'), may hold values from -0.21875 to 0.21875
- w_key: bfloat16 [2, 768, 768], P(None, None, 'mp'), may hold values from -0.21875 to 0.21875
- w_value: bfloat16 [2, 768, 768], P(None, None, 'mp'), may hold values from -0.21875 to 0.21875
- w_output: bfloat16 [2, 768, 768], P(None, None, 'mp'), may hold values from -1.25 to 1.25
- w_inner: bfloat16 [2, 768, 3072], P(None, None, 'mp'), may hold values from -0.21875 to 0.21875
- w_outer: bfloat16 [2, 768, 3072], P(None, None, 'mp'), may hold values from -0.109375 to 0.109375
- norm_gain: float32 [2, 768, 2], replicated, may hold values from 0.5 to 1.5
- norm_bias: float32 [2, 768, 2], replicated, may hold values from -3 to 3
- grad_output: float32 [4, 512, 768], P('dp', 'seq'), may hold values from -6 to 6
- grad_bounds: float32 [4, 16, 2, 768], P('dp', 'seq'), may hold values from -6 to 6
Outputs:
- outputs: float32 [4, 512, 768], P('dp', 'seq')
- bound_rows: float32 [4, 16, 2, 768], P('dp', 'seq')
- grad_inputs: float32 [4, 512, 768], P('dp', 'seq')
- grad_mask: float32 [1, 768], P(None, ('dp', 'seq'))
- grad_query: float32 [2, 768, 768], P(None, ('dp', 'seq'), 'mp')
- grad_key: float32 [2, 768, 768], P(None, ('dp', 'seq'), 'mp')
- grad_value: float32 [2, 768, 768], P(None, ('dp', 'seq'), 'mp')
- grad_w_output: float32 [2, 768, 768], P(None, ('dp', 'seq'), 'mp')
- grad_inner: float32 [2, 768, 3072], P(None, ('dp', 'seq'), 'mp')
- grad_outer: float32 [2, 768, 3072], P(None, ('dp', 'seq'), 'mp')
- grad_gain: float32 [2, 768, 2], P(None, ('dp', 'seq'))
- grad_bias: float32 [2, 768, 2], P(None, ('dp', 'seq'))
The draws below stay inside these ranges and needn't reach their ends.
Inputs may be any that keep to these rules, and one draw needn't show every extreme that they name: span_info[r, s] = (start, length) of span s of row r. Span s starts at or after max(s * 32, 1) and start + length is at most min((s + 1) * 32, 511). Spans never touch: the row just before and just after each span is unmasked. At each border between two blocks of 128 tokens, either the later block's first span starts on the border or the earlier block's last span ends on it, so that the border rows lie on the other side; which of the two, alternates with the row and the border. Lengths run from 1 to 10; every row has a span of exactly 10 tokens.
All inputs are finite; a program needn't handle non-finite values.
Results may differ from the reference program's by a relative error of at most 0.025.
Values may be sent and summed in bfloat16 or wider, within the bound.
No kernel may reach another device: no remote copies, remote signals or barrier semaphores. Data moves between devices by JAX's collectives and lax.ppermute only.
A program may use at most 192 MiB of HBM per device.

```python
import math
import jax
import jax.numpy as jnp
from jax import lax

D = 768
HEADS = 12
HD = 64
FF = 3072
LAYERS = 2
SEQ_LEN = 512
SEG = 32
MAXLEN = 10
ROWS = 4
TOK_SEQ = 128
NSPAN = 16


def draw_span_info(key, part):
    key = jax.random.fold_in(key, 7)
    key_flip = jax.random.fold_in(key, 1)
    key_long = jax.random.fold_in(key, 2)
    key_place = jax.random.fold_in(key, 3)
    span_count = SEQ_LEN // SEG
    per_block = TOK_SEQ // SEG
    block_count = SEQ_LEN // TOK_SEQ
    coin_flips = jax.random.randint(key_flip, (ROWS, span_count, MAXLEN - 1), 0, 5)
    keep_going = jnp.cumprod((coin_flips != 0).astype(jnp.int32), axis=-1)
    lengths = 1 + jnp.sum(keep_going, axis=-1)
    longest = jax.random.randint(key_long, (ROWS, 1), 0, span_count)
    span_slots = jnp.arange(span_count, dtype=jnp.int32)
    lengths = jnp.where(span_slots[None, :] == longest, MAXLEN, lengths)
    seg_start = span_slots * SEG
    row_ids = jnp.arange(ROWS, dtype=jnp.int32)[:, None]
    block_ids = (span_slots // per_block)[None, :]
    lowest = jnp.maximum(seg_start, 1)[None, :]
    upper_end = jnp.minimum(seg_start + SEG, SEQ_LEN - 1)[None, :]
    lower_shift = jnp.where((block_ids > 0) & ((block_ids + row_ids) % 2 == 1), 1, 0)
    upper_cut = jnp.where((block_ids + 1 < block_count) & ((block_ids + 1 + row_ids) % 2 == 0), 1, 0)
    low_limit = lowest + 1
    high_limit = upper_end - 1
    free_room = high_limit - lengths - low_limit
    offsets = jax.random.randint(key_place, (ROWS, span_count), 0, free_room + 1)
    slot_index = (span_slots % per_block)[None, :]
    starts = jnp.where(slot_index == 0, lowest + lower_shift, jnp.where(slot_index == per_block - 1, upper_end - upper_cut - lengths, low_limit + offsets))
    return jnp.stack([starts, lengths], axis=-1).astype(jnp.int32)


def spiked(result, key, source, target, blocks, factor):
    def block_of(axis_at):
        return (jnp.arange(result.shape[axis_at]) // (result.shape[axis_at] // blocks)).reshape((-1,) + (1,) * (result.ndim - 1 - axis_at))

    near = jax.random.permutation(key, blocks)[block_of(target)]
    far = (block_of(target) + blocks // 2) % blocks
    return jnp.where((block_of(source) == near) | (block_of(source) == far), factor * result, result)


def steps_of(own_key, dims, cuts, least, largest):
    loudness = 1.0
    for dim, parts in cuts:
        steps = jax.random.uniform(jax.random.fold_in(jax.random.fold_in(own_key, 6), dim), (parts,), jnp.float32, least / len(cuts), largest / len(cuts))
        loudness = loudness * jnp.repeat(jnp.exp(steps), dims[dim] // parts).reshape((-1,) + (1,) * (len(dims) - 1 - dim))
    return loudness


def normal_values(own_key, dims, scale, reach, cuts=(), held_as=jnp.bfloat16):
    drawn = scale * jax.random.normal(own_key, dims, jnp.float32)
    if cuts:
        drawn = drawn * steps_of(own_key, dims, cuts, -0.22, 0.18)
    return jnp.clip(drawn, -reach, reach).astype(held_as)


def noise_with(rng, extent, scale, reach, cuts, heavy, kind=jnp.bfloat16):
    result = scale * jax.random.normal(rng, extent, jnp.float32)
    if cuts:
        result = result * steps_of(rng, extent, cuts, -0.22, 0.18)
    return jnp.clip(spiked(result, jax.random.fold_in(rng, 3), *heavy), -reach, reach).astype(kind)


def setup_inputs(seed: int = 0) -> dict:
    seeds = jax.random.split(jax.random.key(seed), 14)
    inputs = noise_with(seeds[0], (ROWS, SEQ_LEN, D), 1.0, 6.0, ((0, 4), (1, 4)), (0, 2, 4, 2.0), jnp.float32)
    span_info = draw_span_info(jax.random.fold_in(seeds[13], 71), 0)
    mask_vector = normal_values(seeds[2], (D,), 1.0, 5.0, (), jnp.float32)
    w_query = normal_values(seeds[3], (LAYERS, D, D), D ** -0.5, 0.21875, ((2, 2),))
    w_key = normal_values(seeds[4], (LAYERS, D, D), D ** -0.5, 0.21875, ((2, 2),))
    w_value = normal_values(seeds[5], (LAYERS, D, D), D ** -0.5, 0.21875, ((2, 2),))
    w_output = normal_values(seeds[6], (LAYERS, D, D), (D // 32) ** -0.5, 1.25, ((2, 2),))
    w_inner = normal_values(seeds[7], (LAYERS, D, FF), D ** -0.5, 0.21875, ((2, 2),))
    w_outer = normal_values(seeds[8], (LAYERS, D, FF), FF ** -0.5, 0.109375, ((2, 2),))
    norm_gain = jnp.clip(1.0 + 0.1 * jax.random.normal(seeds[9], (LAYERS, D, 2), jnp.float32), 0.5, 1.5)
    norm_bias = normal_values(seeds[10], (LAYERS, D, 2), 0.5, 3.0, (), jnp.float32)
    grad_output = normal_values(seeds[11], (ROWS, SEQ_LEN, D), 1.0, 6.0, ((0, 4), (1, 4)), jnp.float32)
    grad_bounds = normal_values(seeds[12], (ROWS, NSPAN, 2, D), 1.0, 6.0, ((0, 4), (1, 4)), jnp.float32)
    return {"inputs": inputs, "span_info": span_info, "mask_vector": mask_vector, "w_query": w_query, "w_key": w_key, "w_value": w_value, "w_output": w_output, "w_inner": w_inner, "w_outer": w_outer, "norm_gain": norm_gain, "norm_bias": norm_bias, "grad_output": grad_output, "grad_bounds": grad_bounds}


@jax.custom_vjp
def low(v):
    return lax.optimization_barrier(v.astype(jnp.bfloat16)).astype(jnp.float32)

@jax.custom_vjp
def low_back(v):
    return v

def low_keep(v):
    return (low(v), None)

def low_pass(kept, grad):
    return (grad,)

def back_keep(v):
    return (v, None)

def back_low(kept, grad):
    return (low(grad),)
low.defvjp(low_keep, low_pass)
low_back.defvjp(back_keep, back_low)
eps_norm = 1e-12
highest = lax.Precision.HIGHEST

def layer_norm(values, gain_col, bias_col):
    centre = lax.optimization_barrier(jnp.mean(values, axis=-1, keepdims=True))
    shifted = values - centre
    spread = lax.optimization_barrier(jnp.mean(shifted * shifted, axis=-1, keepdims=True))
    return shifted * lax.rsqrt(spread + eps_norm) * gain_col + bias_col

def attend_row(triple):
    queries, key_rows, value_rows = triple
    scores = jnp.einsum('qhd,khd->hqk', queries, key_rows, precision=highest) * HD ** (-0.5)
    attn_probs = jax.nn.softmax(low_back(scores), axis=-1)
    return jnp.einsum('hqk,khd->qhd', low(attn_probs), value_rows, precision=highest)

def one_layer(hidden, w_query, w_key, w_value, w_output, w_inner, w_outer, gain_cols, bias_cols):
    row_count, seq_count = (hidden.shape[0], hidden.shape[1])
    lowered = low(hidden)

    def project(weight):
        product = jnp.einsum('rld,de->rle', lowered, weight, precision=highest)
        return low(low_back(product)).reshape(row_count, seq_count, HEADS, HD)
    queries, key_rows, value_rows = (project(w_query), project(w_key), project(w_value))
    mixed_heads = lax.map(jax.checkpoint(attend_row), (queries, key_rows, value_rows))
    mixed_heads = low(low_back(mixed_heads.reshape(row_count, seq_count, D)))
    branch = low_back(jnp.einsum('rle,de->rld', mixed_heads, w_output, precision=highest))
    normed = layer_norm(hidden + branch, gain_cols[:, 0], bias_cols[:, 0])
    inner_act = low_back(jnp.einsum('rld,df->rlf', low(normed), w_inner, precision=highest))
    active = low(jax.nn.gelu(inner_act, approximate=False))
    outer_sum = low_back(jnp.einsum('rlf,df->rld', active, w_outer, precision=highest))
    return layer_norm(normed + outer_sum, gain_cols[:, 1], bias_cols[:, 1])

def masked_input(inputs, span_info, mask_vector):
    positions = jnp.arange(inputs.shape[1], dtype=jnp.int32)
    starts = span_info[..., 0]
    span_ends = starts + span_info[..., 1]
    inside = (positions[None, :, None] >= starts[:, None, :]) & (positions[None, :, None] < span_ends[:, None, :])
    masked = jnp.any(inside, axis=-1)[..., None]
    return jnp.where(masked, mask_vector, inputs)

def reference(inputs, span_info, mask_vector, w_query, w_key, w_value, w_output, w_inner, w_outer, norm_gain, norm_bias, grad_output, grad_bounds):
    group_rows = math.gcd(ROWS, max(1, 4096 // SEQ_LEN))
    group_count = ROWS // group_rows
    span_groups = span_info.reshape(group_count, group_rows, NSPAN, 2)

    def forward(inputs, mask_vector, w_query, w_key, w_value, w_output, w_inner, w_outer, norm_gain, norm_bias):

        def group_pass(block_pair):
            row_block, span_block = block_pair
            hidden = masked_input(row_block, span_block, mask_vector)
            for layer_index in range(LAYERS):
                hidden = one_layer(hidden, w_query[layer_index], w_key[layer_index], w_value[layer_index], w_output[layer_index], w_inner[layer_index], w_outer[layer_index], norm_gain[layer_index], norm_bias[layer_index])
            edge_index = jnp.stack([span_block[..., 0] - 1, span_block[..., 0] + span_block[..., 1]], axis=-1)
            edge_index = edge_index.reshape(group_rows, 2 * NSPAN).astype(jnp.int32)
            picked = jnp.take_along_axis(hidden, edge_index[..., None], axis=1)
            return (hidden, picked.reshape(group_rows, NSPAN, 2, D))
        row_groups = inputs.reshape(group_count, group_rows, SEQ_LEN, D)
        outputs, bound_rows = lax.map(jax.checkpoint(group_pass), (row_groups, span_groups))
        return (outputs.reshape(ROWS, SEQ_LEN, D), bound_rows.reshape(ROWS, NSPAN, 2, D))
    float_args = (inputs, mask_vector) + tuple((matrix.astype(jnp.float32) for matrix in (w_query, w_key, w_value, w_output, w_inner, w_outer))) + (norm_gain, norm_bias)
    primal, pullback = jax.vjp(forward, *float_args)
    gradients = pullback((grad_output, grad_bounds))
    outputs, bound_rows = primal
    return (outputs, bound_rows, gradients[0], gradients[1].reshape(1, D), gradients[2], gradients[3], gradients[4], gradients[5], gradients[6], gradients[7], gradients[8], gradients[9])
```

```python
import jax
import jax.numpy as jnp
from jax import lax
from jax.sharding import PartitionSpec as P

HD = 64
LAYERS = 2
EPS = 1e-12
BF = jnp.bfloat16
F32 = jnp.float32


def dot(a, b, ca, cb):
    return lax.dot_general(a, b, (((ca,), (cb,)), ((), ())), preferred_element_type=F32)


def norm_parts(a):
    mu = jnp.mean(a, axis=-1, keepdims=True)
    sh = a - mu
    rstd = lax.rsqrt(jnp.mean(sh * sh, axis=-1, keepdims=True) + EPS)
    return sh * rstd, rstd


def norm_back(grad, n, rstd, gain):
    e = grad * gain
    ga = (e - jnp.mean(e, axis=-1, keepdims=True) - n * jnp.mean(e * n, axis=-1, keepdims=True)) * rstd
    return ga, jnp.sum(grad * n, axis=0), jnp.sum(grad, axis=0)


def flip(x, axis, bit):
    count = lax.axis_size(axis)
    return lax.ppermute(x, axis, [(i, i ^ bit) for i in range(count)])


def gather_group(x):
    n = lax.axis_size("seq")
    return [x] + [flip(x, "seq", j) for j in range(1, n)]


def heads(x):
    return x.reshape(x.shape[0], -1, HD)


def layer_forward(hidden, W, gains, biases):
    wq, wk, wv, wo, wi, wu = W
    low = hidden.astype(BF)
    half = wk.shape[1] // 2
    k = dot(low, wk, 1, 0).astype(BF)
    v = dot(low, wv, 1, 0).astype(BF)
    kp, vp = flip(k, "mp", 1), flip(v, "mp", 1)
    q = dot(low, wq, 1, 0).astype(BF)

    def join(a, b):
        b = jnp.concatenate([b[:, half:], b[:, :half]], axis=1)
        return jnp.concatenate([a, b], axis=0)

    ka, va = join(k, kp), join(v, vp)
    s = jnp.einsum("qhd,khd->hqk", heads(q), heads(ka), preferred_element_type=F32) * HD**-0.5
    s = s - jnp.max(s, axis=-1, keepdims=True)
    e = jnp.exp(s)
    probs = e / jnp.sum(e, axis=-1, keepdims=True)
    lp = probs.astype(BF)
    mixed = jnp.einsum("hqk,khd->qhd", lp, heads(va), preferred_element_type=F32)
    mixed = mixed.reshape(low.shape).astype(BF)
    branch = dot(mixed, wo, 1, 1)
    n1, r1 = norm_parts(hidden + branch)
    normed = n1 * gains[:, 0] + biases[:, 0]
    ln = normed.astype(BF)
    inner = dot(ln, wi, 1, 0)
    cdf = 0.5 * (1.0 + lax.erf(inner * 0.7071067811865476))
    act = (inner * cdf).astype(BF)
    dgelu = (cdf + inner * jnp.exp(-0.5 * inner * inner) * 0.3989422804014327).astype(BF)
    outer = dot(act, wu, 1, 1)
    n2, r2 = norm_parts(normed + outer)
    result = n2 * gains[:, 1] + biases[:, 1]
    return result, (low, q, ka, va, lp, mixed, n1, r1, ln, act, dgelu, n2, r2)


def layer_backward(grad, stored, W, gains, sel):
    wq, wk, wv, wo, wi, wu = W
    low, q, ka, va, lp, mixed, n1, r1, ln, act, dgelu, n2, r2 = stored
    t = low.shape[0]
    half = wk.shape[1] // 2
    gmid, gg2, gb2 = norm_back(grad, n2, r2, gains[:, 1])
    lmid = gmid.astype(BF)
    gact = dot(lmid, wu, 1, 0)
    linner = (gact * dgelu.astype(F32)).astype(BF)
    pick_mid = dot(sel, lmid, 1, 1).astype(BF)
    pick_ln = dot(sel, ln, 1, 1).astype(BF)
    g_outer = dot(pick_mid, act, 1, 0)
    g_inner = dot(pick_ln, linner, 1, 0)
    gnormed = gmid + dot(linner, wi, 1, 1)
    gres, gg1, gb1 = norm_back(gnormed, n1, r1, gains[:, 0])
    lres = gres.astype(BF)
    gmix = dot(lres, wo, 1, 0).astype(BF)
    pick_res = dot(sel, lres, 1, 1).astype(BF)
    g_wo = dot(pick_res, mixed, 1, 0)
    gp = jnp.einsum("qhd,khd->hqk", heads(gmix), heads(va), preferred_element_type=F32)
    pf = lp.astype(F32)
    ls = (pf * (gp - jnp.sum(pf * gp, axis=-1, keepdims=True))).astype(BF)
    scale = HD**-0.5
    gv = jnp.einsum("hqk,qhd->khd", lp, heads(gmix), preferred_element_type=F32).reshape(2 * t, -1)
    gk = jnp.einsum("hqk,qhd->khd", ls, heads(q), preferred_element_type=F32).reshape(2 * t, -1) * scale
    gkv = jnp.concatenate([gk, gv], axis=1)
    theirs = flip(gkv[t:].astype(BF), "mp", 1)
    gq = (jnp.einsum("hqk,khd->qhd", ls, heads(ka), preferred_element_type=F32) * scale).reshape(t, -1).astype(BF)
    h = half
    theirs = jnp.concatenate([theirs[:, h : 2 * h], theirs[:, :h], theirs[:, 3 * h :], theirs[:, 2 * h : 3 * h]], axis=1)
    gkv = (gkv[:t] + theirs.astype(F32)).astype(BF)
    gk, gv = gkv[:, : 2 * h], gkv[:, 2 * h :]
    pick_low = dot(sel, low, 1, 1).astype(BF)
    g_q, g_k, g_v = dot(pick_low, gq, 1, 0), dot(pick_low, gk, 1, 0), dot(pick_low, gv, 1, 0)
    ghid = gres + dot(gq, wq, 1, 1) + dot(gk, wk, 1, 1) + dot(gv, wv, 1, 1)
    return ghid, (g_outer, g_inner), (g_wo, g_q, g_k, g_v), (gg1, gg2, gb1, gb2)


def reduce_group(parts):
    keep = jnp.concatenate([p[:, : p.shape[1] // 2] for p in parts], axis=1)
    send = jnp.concatenate([p[:, p.shape[1] // 2 :] for p in parts], axis=1)
    keep = keep + flip(send.astype(BF), "mp", 1).astype(F32)
    bit = 1
    while bit < lax.axis_size("dp"):
        n = keep.shape[0] // 2
        keep = keep[:n] + flip(keep[n:].astype(BF), "dp", bit).astype(F32)
        bit *= 2
    sizes = [p.shape[1] // 2 for p in parts]
    out, at = [], 0
    for w in sizes:
        out.append(keep[:, at : at + w])
        at += w
    return out


def on_device(inputs, span_info, mask_vector, w_query, w_key, w_value, w_output, w_inner, w_outer, norm_gain, norm_bias, grad_output, grad_bounds):
    t, d = inputs.shape[1:]
    ns, nd = lax.axis_size("seq"), lax.axis_size("dp")
    s, z, m = lax.axis_index("seq"), lax.axis_index("dp"), lax.axis_index("mp")
    hrows = t // 2

    def mine(x):
        return lax.dynamic_slice_in_dim(x[0], m * hrows, hrows, 0)

    starts, ends = span_info[0, :, 0], span_info[0, :, 0] + span_info[0, :, 1]
    place = s * t + m * hrows + jnp.arange(hrows, dtype=jnp.int32)
    masked = jnp.any((place[:, None] >= starts) & (place[:, None] < ends), axis=1)[:, None]
    hid = jnp.where(masked, mask_vector, mine(inputs))
    low0 = hid.astype(BF)
    hidden = jnp.concatenate([hid] + [b.astype(F32) for b in gather_group(low0)[1:]], axis=0)
    edges = jnp.stack([starts - 1, ends], axis=-1).reshape(-1)
    all_edges = jnp.concatenate(gather_group(edges))
    all_marks = jnp.concatenate(gather_group(masked.astype(F32)))
    both = jnp.concatenate([mine(grad_output), grad_bounds.reshape(-1, d)], axis=0)
    got = gather_group(both)
    places = jnp.concatenate([place + ((s ^ j) - s) * t for j in range(ns)])
    onehot = (places[:, None] == all_edges[None, :]).astype(F32)
    bounds = jnp.concatenate([g[hrows:] for g in got])
    grad = jnp.concatenate([g[:hrows] for g in got]) + jnp.dot(onehot, bounds, precision=lax.Precision.HIGHEST)

    order = [0]
    bit = 1
    while bit < nd:
        order = order + [o + bit for o in order]
        bit *= 2
    order = [int(bin(i + nd)[3:][::-1], 2) if nd > 1 else 0 for i in range(nd)]
    per = d // (ns * nd)
    base = jnp.concatenate([((z ^ o) * ns + s) * per + jnp.arange(per, dtype=jnp.int32) for o in order])
    sel = (base[:, None] == jnp.arange(d, dtype=jnp.int32)[None, :]).astype(BF)

    weights = []
    for i in range(LAYERS):
        weights.append([jnp.concatenate([w[i], flip(w[i], "mp", 1)], axis=1) for w in (w_query, w_key, w_value, w_output, w_inner, w_outer)])
    kept = []
    for i in range(LAYERS):
        hidden, st = layer_forward(hidden, weights[i], norm_gain[i], norm_bias[i])
        kept.append(st)
    mine_out = hidden[:hrows]
    other_out = flip(mine_out, "mp", 1)
    outputs = jnp.where(m == 0, jnp.concatenate([mine_out, other_out]), jnp.concatenate([other_out, mine_out]))[None]
    pick = (edges[:, None] == places[None, :]).astype(F32)
    rows = jnp.dot(pick, hidden, precision=lax.Precision.HIGHEST)
    rows = rows + flip(rows, "mp", 1)
    bound_rows = rows.reshape(1, -1, 2, d)
    big, vecs = [None] * LAYERS, [None] * LAYERS
    for i in reversed(range(LAYERS)):
        grad, ffn, att, vecs[i] = layer_backward(grad, kept[i], weights[i], norm_gain[i], sel)
        big[i] = reduce_group(ffn), reduce_group(att)
    g_own = jnp.where(masked, 0.0, grad[:hrows])
    g_oth = flip(g_own, "mp", 1)
    grad_inputs = jnp.where(m == 0, jnp.concatenate([g_own, g_oth]), jnp.concatenate([g_oth, g_own]))[None]
    gmask = jnp.sum(grad * all_marks, axis=0)
    small = jnp.stack([gmask] + [vecs[i][j] for i in range(LAYERS) for j in range(4)], axis=1)
    small = small + flip(small, "mp", 1)
    small = jnp.dot(sel.astype(F32), small, precision=lax.Precision.HIGHEST)
    bit = 1
    while bit < nd:
        n = small.shape[0] // 2
        small = small[:n] + flip(small[n:], "dp", bit)
        bit *= 2
    vec = small[:, 1:].reshape(per, LAYERS, 4).transpose(1, 0, 2)
    st = lambda a, b: jnp.stack([big[i][a][b] for i in range(LAYERS)])
    return (
        outputs,
        bound_rows,
        grad_inputs,
        small[:, 0][None],
        st(1, 1),
        st(1, 2),
        st(1, 3),
        st(1, 0),
        st(0, 1),
        st(0, 0),
        vec[..., 0:2],
        vec[..., 2:4],
    )


def solution(mesh):
    row = P("dp", "seq", None)
    wide = P(None, None, "mp")
    out_w = P(None, ("dp", "seq"), "mp")
    out_v = P(None, ("dp", "seq"), None)
    return jax.shard_map(
        on_device,
        mesh=mesh,
        in_specs=(row, row, P(), wide, wide, wide, wide, wide, wide, P(), P(), row, P("dp", "seq", None, None)),
        out_specs=(row, P("dp", "seq", None, None), row, P(None, ("dp", "seq"))) + (out_w,) * 6 + (out_v,) * 2,
        check_vma=False,
    )
```

```python
import jax
import jax.numpy as jnp
from jax import lax
from jax.experimental import pallas as pl
from jax.experimental.pallas import tpu as pltpu
from jax.sharding import PartitionSpec as P

HD = 64
LAYERS = 2
EPS = 1e-12
SCALE = HD**-0.5
BF = jnp.bfloat16
F32 = jnp.float32
I32 = jnp.int32
LANES = 128
LIMIT = 8 * 2**20
TOP = 10
RATE = 0.3e9
GROUP = 6
VM = pl.BlockSpec(memory_space=pltpu.VMEM)
SM = pl.BlockSpec(memory_space=pltpu.SMEM)
HB = pl.BlockSpec(memory_space=pltpu.HBM)


def shape(dims, kind=F32):
    return jax.ShapeDtypeStruct(tuple(dims), kind)


def run(body, outs, *args, name=None, smem=0, hbm=0, scratch=(), out_specs=None, limit=LIMIT, us=1.0, after=()):
    specs = [SM] * smem + [VM] * (len(args) - smem - hbm) + [HB] * hbm + [pl.BlockSpec(memory_space=pl.ANY)] * len(after)
    count = len(args)
    args = args[: len(args) - hbm] + tuple(pltpu.with_memory_space_constraint(a, pltpu.HBM) for a in args[len(args) - hbm :])
    def whole(*refs):
        body(*refs[:count], *refs[count + len(after) :])

    return pl.pallas_call(
        whole,
        out_shape=tuple(outs),
        in_specs=specs,
        out_specs=(VM,) * len(outs) if out_specs is None else tuple(out_specs),
        scratch_shapes=scratch,
        compiler_params=pltpu.CompilerParams(vmem_limit_bytes=limit),
        cost_estimate=pl.CostEstimate(flops=int(us * RATE), bytes_accessed=1, transcendentals=0),
        name=name,
    )(*args, *after)


def dot(a, b, ca, cb):
    return lax.dot_general(a, b, (((ca,), (cb,)), ((), ())), preferred_element_type=F32)


def flip(x, axis, mask):
    count = lax.axis_size(axis)
    return lax.ppermute(x, axis, [(i, i ^ mask) for i in range(count)])


def fetch(layer, sources, buffers, sems, first=0):
    copies = []
    for i, (w, b) in enumerate(zip(sources, buffers)):
        c = pltpu.make_async_copy(w.at[layer], b, sems.at[first + i])
        c.start()
        copies.append(c)
    return copies


def own_place(own):
    return lax.axis_index("seq") * (2 * own) + lax.axis_index("mp") * own


def first_body(spans, mask_vector, inputs, grads, bounds, low, payload, hid, mv, gv, bv, sems):
    own, d = low.shape
    n = spans.shape[1]
    at = lax.axis_index("mp") * own
    copies = [
        pltpu.make_async_copy(inputs.at[0, pl.ds(at, own)], hid, sems.at[0]),
        pltpu.make_async_copy(mask_vector, mv.at[0], sems.at[1]),
        pltpu.make_async_copy(grads.at[0, pl.ds(at, own)], gv, sems.at[2]),
        pltpu.make_async_copy(bounds.at[0], bv, sems.at[3]),
    ]
    for c in copies:
        c.start()
    pos = lax.broadcasted_iota(I32, (own, 1), 0) + own_place(own)
    lane = lax.broadcasted_iota(I32, (8, d), 1) % (2 * n)
    mask = pos < 0
    edges = jnp.zeros((8, d), I32)
    for i in range(n):
        a, e = spans[0, i, 0], spans[0, i, 0] + spans[0, i, 1]
        mask = mask | ((pos >= a) & (pos < e))
        edges = jnp.where(lane == 2 * i, a - 1, jnp.where(lane == 2 * i + 1, e, edges))
    upper = lax.broadcasted_iota(I32, (8, d), 0) < 4
    edges = jnp.where(upper, edges // 16, edges % 16).astype(F32)
    copies[0].wait()
    copies[1].wait()
    x = jnp.where(mask, mv[...], hid[...])
    low[...] = x.astype(BF)
    copies[2].wait()
    copies[3].wait()
    payload[0:own] = gv[...].astype(BF)
    payload[own:] = jnp.concatenate([bv[i] for i in range(n)] + [edges], axis=0).astype(BF)


def kv_first_body(*refs):
    parts, (wkm, wko, wvm, wvo, hid, low, k, v) = refs[:-8], refs[-8:]
    r = parts[0].shape[0]
    for i, p in enumerate(parts):
        sl = slice(i * r, (i + 1) * r)
        hid[sl] = p[...].astype(F32)
        low[sl] = p[...]
    keys_values(low[...], (wkm, wko, wvm, wvo), k, v)


def keys_values(x, ws, k, v):
    h = ws[0].shape[1]
    for out, pair in ((k, ws[:2]), (v, ws[2:])):
        for i, w in enumerate(pair):
            out[:, i * h : (i + 1) * h] = dot(x, w[...], 1, 0).astype(BF)


def q_body(low, wqm, wqo, q):
    h = wqm.shape[1]
    x = low[...]
    for i, w in enumerate((wqm, wqo)):
        q[:, i * h : (i + 1) * h] = (dot(x, w[...], 1, 0) * SCALE).astype(BF)


def halves_of_pair():
    lanes = lax.broadcasted_iota(I32, (1, LANES), 1) < HD
    rows = lax.broadcasted_iota(I32, (LANES, 1), 0) < HD
    return lanes, rows


def rows_of(own, oth, g):
    pairs = own.shape[1] // LANES
    g2 = (g + pairs // 2) % pairs
    return jnp.concatenate([own[:, g * LANES : (g + 1) * LANES], oth[:, g2 * LANES : (g2 + 1) * LANES]], axis=0)


def normalize(a):
    mu = jnp.mean(a, axis=-1, keepdims=True)
    sh = a - mu
    rstd = lax.rsqrt(jnp.mean(sh * sh, axis=-1, keepdims=True) + EPS)
    return sh * rstd, rstd


def attend(q, k, v, ko, vo, probs, mixed):
    width = q.shape[1]
    pairs = width // LANES
    lo, top = halves_of_pair()
    for g0 in range(0, pairs, GROUP):
        scores = []
        for g in range(g0, g0 + GROUP):
            qq = q[:, g * LANES : (g + 1) * LANES]
            kk = rows_of(k, ko, g)
            scores += [dot(kk, jnp.where(m, qq, 0), 1, 1) for m in (lo, ~lo)]
        exps = [jnp.exp(s - jnp.max(s, axis=0, keepdims=True)) for s in scores]
        low = [(e * (1.0 / jnp.sum(e, axis=0, keepdims=True))).astype(BF) for e in exps]
        for j in range(2 * GROUP):
            probs[2 * g0 + j] = low[j]
        for g in range(g0, g0 + GROUP):
            j = 2 * (g - g0)
            vv = rows_of(v, vo, g)
            r = jnp.where(top, dot(vv, low[j], 0, 0), dot(vv, low[j + 1], 0, 0))
            mixed[:, g * LANES : (g + 1) * LANES] = r.T.astype(BF)


def attend_out(hid, mixed, wom, woo, gain, bias, n1, r1, ln):
    h = wom.shape[1]
    branch = dot(mixed[:, :h], wom[...], 1, 1) + dot(mixed[:, h:], woo[...], 1, 1)
    n, r = normalize(hid[...] + branch)
    n1[...] = n
    r1[...] = r
    y = n * gain + bias
    ln[...] = y.astype(BF)
    return y


def ffn_half(x, i, wi, wu, act, dgelu):
    f = wi.shape[1]
    inner = dot(x, wi[...], 1, 0)
    cdf = 0.5 + 0.5 * lax.erf(inner * 0.7071067811865476)
    a = (inner * cdf).astype(BF)
    act[:, i * f : (i + 1) * f] = a
    dgelu[:, i * f : (i + 1) * f] = (cdf + inner * jnp.exp(-0.5 * inner * inner) * 0.3989422804014327).astype(BF)
    return dot(a, wu[...], 1, 1)


def norm_back(grad, n, rstd, gain):
    e = grad * gain
    back = (e - jnp.mean(e, axis=-1, keepdims=True) - n * jnp.mean(e * n, axis=-1, keepdims=True)) * rstd
    return back, jnp.sum(grad * n, axis=0, keepdims=True), jnp.sum(grad, axis=0, keepdims=True)


def weight_grad(sel, a, bs, keep, send, at=0):
    pick = dot(sel[...], a[...], 1, 1).astype(BF)
    for b in bs:
        h = b.shape[1] // 2
        keep[:, at : at + h] = dot(pick, b[:, :h], 1, 0)
        send[:, at : at + h] = dot(pick, b[:, h:], 1, 0).astype(BF)
        at += h


def fetch_layer(layer, wom, woo, wim, wio, wum, wuo, bufs, sems):
    pairs = zip((wom, woo, wim, wum, wio, wuo), (0, 1, 2, 4, 3, 5))
    copies = [None] * 6
    for w, i in pairs:
        copies[i] = pltpu.make_async_copy(w.at[layer], bufs[i], sems.at[i])
        copies[i].start()
    return copies


def ffn(y, ln, copies, bufs, act, dgelu):
    x = ln[...]
    for i in range(2):
        copies[2 + i].wait()
        copies[4 + i].wait()
        y = y + ffn_half(x, i, bufs[2 + i], bufs[4 + i], act, dgelu)
    return normalize(y)


def forward_body(q, k, v, ko, vo, hid, gains, biases, wom, woo, wim, wio, wum, wuo, wkm, wko, wvm, wvo, wqm, wqo,
                 probs, mixed, n1, r1, ln, act, dgelu, n2, r2, hid2, low2, k2, v2, bom, boo, bim, bio, bum, buo,
                 bkm, bko, bvm, bvo, bqm, bqo, sems):
    bufs = (bom, boo, bim, bio, bum, buo)
    copies = fetch_layer(0, wom, woo, wim, wio, wum, wuo, bufs, sems)
    copies += fetch(1, (wkm, wko, wvm, wvo, wqm, wqo), (bkm, bko, bvm, bvo, bqm, bqo), sems, 6)
    attend(q, k, v, ko, vo, probs, mixed)
    copies[0].wait()
    copies[1].wait()
    y = attend_out(hid, mixed, bufs[0], bufs[1], gains[0, 0:1], biases[0, 0:1], n1, r1, ln)
    n, r = ffn(y, ln, copies, bufs, act, dgelu)
    n2[...] = n
    r2[...] = r
    y = n * gains[0, 1:2] + biases[0, 1:2]
    hid2[...] = y
    low = y.astype(BF)
    low2[...] = low
    for c in copies[6:]:
        c.wait()
    keys_values(low, (bkm, bko, bvm, bvo), k2, v2)


def turn_body(q, k, v, ko, vo, hid, gains, biases, grad, sel, wom, woo, wim, wio, wum, wuo,
              probs, mixed, n1, r1, ln, dgelu, hid2, mid, lmid, vec, keep, send, bom, boo, bim, bio, bum, buo, act, sems):
    bufs = (bom, boo, bim, bio, bum, buo)
    copies = fetch_layer(1, wom, woo, wim, wio, wum, wuo, bufs, sems)
    attend(q, k, v, ko, vo, probs, mixed)
    copies[0].wait()
    copies[1].wait()
    y = attend_out(hid, mixed, bufs[0], bufs[1], gains[1, 0:1], biases[1, 0:1], n1, r1, ln)
    n, r = ffn(y, ln, copies, bufs, act, dgelu)
    hid2[...] = n * gains[1, 1:2] + biases[1, 1:2]
    middle_back(grad[...], n, r, gains[1, 1:2], mid, lmid, vec)
    weight_grad(sel, lmid, (act,), keep, send)


def middle_back(grad, n, r, gain, mid, lmid, vec):
    back, gg, gb = norm_back(grad, n, r, gain)
    mid[...] = back
    lmid[...] = back.astype(BF)
    vec[0:1] = gg
    vec[1:2] = gb


def ffn_back_body(layer):
    def body(mid, lmid, dgelu, gains, n1, r1, wom, woo, wim, wio, wum, wuo, inner, res, lres, mix, vec):
        f = wim.shape[1]
        x = lmid[...]
        total = mid[...]
        for i, (wi, wu) in enumerate(((wim, wum), (wio, wuo))):
            g = (dot(x, wu[...], 1, 0) * dgelu[:, i * f : (i + 1) * f].astype(F32)).astype(BF)
            inner[:, i * f : (i + 1) * f] = g
            total = total + dot(g, wi[...], 1, 1)
        back, gg, gb = norm_back(total, n1[...], r1[...], gains[layer, 0:1])
        res[...] = back
        low = back.astype(BF)
        lres[...] = low
        vec[0:1] = gg
        vec[1:2] = gb
        h = wom.shape[1]
        mix[:, :h] = dot(low, wom[...], 1, 0).astype(BF)
        mix[:, h:] = dot(low, woo[...], 1, 0).astype(BF)

    return body


def grad_one_body(sel, a, b, keep, send):
    weight_grad(sel, a, (b,), keep, send)


def attend_back_body(mix, mixed, probs, q, v, vo, dscores, dk, dv):
    t, width = q.shape
    pairs = width // LANES
    lo, top = halves_of_pair()
    for g in range(pairs):
        sl = slice(g * LANES, (g + 1) * LANES)
        gg = mix[:, sl]
        vv = rows_of(v, vo, g)
        delta = (gg.astype(F32) * mixed[:, sl].astype(F32)).T
        ds = []
        for j, m in enumerate((lo, ~lo)):
            dl = jnp.sum(delta[j * HD : (j + 1) * HD], axis=0, keepdims=True)
            dp = dot(vv, jnp.where(m, gg, 0), 1, 1)
            ds.append((probs[2 * g + j].astype(F32) * (dp - dl)).astype(BF))
            dscores[2 * g + j] = ds[j]
        qq = q[:, sl]
        g2 = (g + pairs // 2) % pairs
        to = slice(g2 * LANES, (g2 + 1) * LANES)
        dk[:, to] = jnp.where(lo, dot(ds[0][t:], qq, 1, 0), dot(ds[1][t:], qq, 1, 0)).astype(BF)
        dv[:, to] = jnp.where(lo, dot(probs[2 * g, t:], gg, 1, 0), dot(probs[2 * g + 1, t:], gg, 1, 0)).astype(BF)


def attend_back_own(mix, probs, dscores, q, k, ko, res, wqm, wqo, dk, dv, gq, part):
    t, width = q.shape
    pairs = width // LANES
    lo, top = halves_of_pair()
    for g in range(pairs):
        sl = slice(g * LANES, (g + 1) * LANES)
        gg, qq = mix[:, sl], q[:, sl]
        kk = rows_of(k, ko, g)
        dq = jnp.where(top, dot(kk, dscores[2 * g], 0, 0), dot(kk, dscores[2 * g + 1], 0, 0))
        gq[:, sl] = (dq * SCALE).T.astype(BF)
        dk[:, sl] = jnp.where(lo, dot(dscores[2 * g, :t], qq, 1, 0), dot(dscores[2 * g + 1, :t], qq, 1, 0))
        dv[:, sl] = jnp.where(lo, dot(probs[2 * g, :t], gg, 1, 0), dot(probs[2 * g + 1, :t], gg, 1, 0))
    h = width // 2
    part[...] = res[...] + dot(gq[:, :h], wqm[...], 1, 1) + dot(gq[:, h:], wqo[...], 1, 1)


def attend_back_load_body(mix, probs, dscores, q, k, ko, res, wqm, wqo, wkm, wko, wvm, wvo, dk, dv, gq, part, *rest):
    (bkm, bko, bvm, bvo, bqm, bqo), sems = rest[:6], rest[6]
    copies = fetch(0, (wqm, wqo, wkm, wko, wvm, wvo), (bqm, bqo, bkm, bko, bvm, bvo), sems)
    for c in copies[:2]:
        c.wait()
    attend_back_own(mix, probs, dscores, q, k, ko, res, bqm, bqo, dk, dv, gq, part)
    for c in copies[2:]:
        c.wait()


def hidden_back(part, dk, dv, dk2, dv2, ws, gk, gv):
    h = ws[0].shape[1]
    total = part[...]
    for own, other, out, pair in ((dk, dk2, gk, ws[:2]), (dv, dv2, gv, ws[2:])):
        for i, w in enumerate(pair):
            sl = slice(i * h, (i + 1) * h)
            g = (own[:, sl] + other[:, sl].astype(F32)).astype(BF)
            out[:, sl] = g
            total = total + dot(g, w[...], 1, 1)
    return total


def next_layer_body(part, dk, dv, dk2, dv2, wkm, wko, wvm, wvo, n2, r2, gains, sel, act, gk, gv, mid, lmid, vec, keep, send):
    grad = hidden_back(part, dk, dv, dk2, dv2, (wkm, wko, wvm, wvo), gk, gv)
    middle_back(grad, n2[...], r2[...], gains[0, 1:2], mid, lmid, vec)
    weight_grad(sel, lmid, (act,), keep, send)


def grad_attention_body(sel, lres, mixed, low, gq, gk, gv, keep, send):
    w = gq.shape[1]
    weight_grad(sel, lres, (mixed,), keep, send)
    weight_grad(sel, low, (gq, gk, gv), keep, send, w // 2)


def split_dot(onehot, x, ca, cb):
    total = None
    for _ in range(3):
        part = x.astype(BF)
        x = x - part.astype(F32)
        y = dot(onehot, part, ca, cb)
        total = y if total is None else total + y
    return total


def last_body(part, dk, dv, dk2, dv2, wkm, wko, wvm, wvo, sel, low, gq, marks, v1, v2, v3, v4, grad_in, keep, send, gk, gv):
    w = gq.shape[1]
    own = grad_in.shape[0]
    grad = hidden_back(part, dk, dv, dk2, dv2, (wkm, wko, wvm, wvo), gk, gv)
    weight_grad(sel, low, (gq, gk, gv), keep, send)
    grad_in[...] = jnp.where(marks[0:own, 0:1] > 0.5, 0.0, grad[0:own])
    mask = jnp.sum(grad * marks[:, 0:1], axis=0, keepdims=True)
    rows = jnp.concatenate([v1[...], v2[...], v3[...], v4[...], jnp.broadcast_to(mask, (8,) + mask.shape[1:])], axis=0)
    rows = jnp.concatenate([rows, jnp.zeros((LANES - rows.shape[0], rows.shape[1]), F32)], axis=0)
    small = split_dot(sel[...], rows, 1, 1)
    keep[:, 3 * w // 2 :] = small
    send[:, 3 * w // 2 :] = small.astype(BF)


def join_body(parts):
    def body(*refs):
        keeps, gots, rest, sends = refs[:parts], refs[parts : 2 * parts], refs[2 * parts], refs[2 * parts + 1 :]
        n, at = rest.shape[0], 0
        for keep, got in zip(keeps, gots):
            to = slice(at, at + keep.shape[1])
            rest[:, to] = keep[0:n] + got[0:n].astype(F32)
            for i, x in enumerate(sends):
                sl = slice((i + 1) * n, (i + 2) * n)
                x[:, to] = (keep[sl] + got[sl].astype(F32)).astype(BF)
            at += keep.shape[1]

    return body


def add_body(keep, got, rest, send):
    n = rest.shape[0]
    rest[...] = keep[0:n] + got[0:n].astype(F32)
    send[...] = (keep[n:] + got[n:].astype(F32)).astype(BF)


def load_body(x, wkm, wko, wvm, wvo, wqm, wqo, y, bkm, bko, bvm, bvo, bqm, bqo, sems):
    copies = fetch(0, (wkm, wko, wvm, wvo, wqm, wqo), (bkm, bko, bvm, bvo, bqm, bqo), sems)
    y[...] = x[...]
    for c in copies:
        c.wait()


def top_body(*refs):
    n = len(refs) - 2
    parts, (grad, marks) = refs[:n], refs[n:]
    h = grad.shape[0] // n
    lane = lax.broadcasted_iota(I32, (1, LANES), 1)
    edges = jnp.full((1, LANES), -8.0, F32)
    bounds = []
    for j, p in enumerate(parts):
        tail = p[h:].astype(F32)
        b = tail.shape[0] - 8
        edges = jnp.where((lane >= j * b) & (lane < (j + 1) * b), edges_of(tail), edges)
        bounds.append(tail[0:b])
    bounds = jnp.concatenate(bounds, axis=0)
    bounds = jnp.concatenate([bounds, jnp.zeros((LANES - bounds.shape[0], bounds.shape[1]), F32)], axis=0).astype(BF)
    row = lax.broadcasted_iota(I32, (h, 1), 0)
    even = (lane % 2) == 0
    for j, p in enumerate(parts):
        pos = (row + block_place(j, h)).astype(F32)
        onehot = jnp.where(pos == edges, 1.0, 0.0).astype(BF)
        grad[j * h : (j + 1) * h] = p[0:h].astype(F32) + dot(onehot, bounds, 1, 0)
        after = jnp.where((even & (pos > edges)) & (edges > -4.0), 1.0, 0.0) - jnp.where((~even & (pos >= edges)) & (edges > -4.0), 1.0, 0.0)
        marks[j * h : (j + 1) * h] = jnp.broadcast_to(jnp.sum(after, axis=1, keepdims=True), (h, LANES))


def block_place(j, own):
    return (lax.axis_index("seq") ^ j) * (2 * own) + lax.axis_index("mp") * own


def edges_of(payload):
    e = payload[-8:, 0:LANES].astype(F32)
    return e[0:1] * 16.0 + e[4:5]


def result_body(hid, payload, out):
    own = hid.shape[0] // lax.axis_size("seq")
    n = out.shape[0] - own
    out[0:own] = hid[0:own]
    row = jnp.broadcast_to(edges_of(payload[own:].astype(F32)), (8, LANES)).T[0:n, 0:1]
    lane = lax.broadcasted_iota(I32, (1, own), 1)
    total = None
    for j in range(hid.shape[0] // own):
        pos = (lane + block_place(j, own)).astype(F32)
        onehot = jnp.where(row == pos, 1.0, 0.0).astype(BF)
        y = split_dot(onehot, hid[j * own : (j + 1) * own], 1, 0)
        total = y if total is None else total + y
    out[own:] = total


def put_body(mine, other, out, bound, rows, sems):
    n = bound.shape[1] * 2
    own = mine.shape[0] - n
    m = lax.axis_index("mp")
    a = pltpu.make_async_copy(mine.at[0:own], out.at[0, pl.ds(m * own, own)], sems.at[0])
    b = pltpu.make_async_copy(other.at[0:own], out.at[0, pl.ds((1 - m) * own, own)], sems.at[1])
    a.start()
    b.start()
    total = mine[own:] + other[own:]
    for i in range(n // 2):
        rows[i] = total[2 * i : 2 * i + 2]
    c = pltpu.make_async_copy(rows, bound.at[0], sems.at[2])
    c.start()
    a.wait()
    b.wait()
    c.wait()


def place_body(mine, other, out, sems):
    own = mine.shape[0]
    m = lax.axis_index("mp")
    a = pltpu.make_async_copy(mine, out.at[0, pl.ds(m * own, own)], sems.at[0])
    b = pltpu.make_async_copy(other, out.at[0, pl.ds((1 - m) * own, own)], sems.at[1])
    a.start()
    b.start()
    a.wait()
    b.wait()


def finish_body(places, width, terms):
    def body(*refs):
        layers, outs = [refs[i * terms : (i + 1) * terms] for i in range(LAYERS)], refs[LAYERS * terms :]

        def total(i, sl):
            x = layers[i][0][:, sl]
            for r in layers[i][1:]:
                x = x + r[:, sl].astype(F32)
            return x

        for i in range(LAYERS):
            for j, at in enumerate(places):
                outs[j][i] = total(i, slice(at[i], at[i] + width))
        if len(outs) > len(places):
            gain, bias, mask = outs[len(places) :]
            small = total(0, slice(3 * width, 3 * width + LANES))
            for i in range(LAYERS):
                for j in range(2):
                    at = 4 * i + 2 * j
                    gain[i, :, j : j + 1] = small[:, at : at + 1]
                    bias[i, :, j : j + 1] = small[:, at + 1 : at + 2]
            mask[...] = small.T[8:9]

    return body


def order_of(masks):
    if not masks:
        return [0]
    rest = order_of(masks[1:])
    return rest + [r ^ masks[0] for r in rest]


def tie(x, *others):
    return lax.optimization_barrier((x,) + others)[0]


def on_device(inputs, span_info, mask_vector, w_query, w_key, w_value, w_output, w_inner, w_outer, norm_gain, norm_bias, grad_output, grad_bounds):
    t, d = inputs.shape[1:]
    ns, nd = lax.axis_size("seq"), lax.axis_size("dp")
    s, z = lax.axis_index("seq"), lax.axis_index("dp")
    f = w_inner.shape[2]
    hw = w_query.shape[2]
    heads = 2 * hw // HD
    own = t // 2
    tok = own * ns
    axes = ("dp", "seq")
    masks = []
    bit = ns
    while bit < ns * nd:
        masks.append(bit)
        bit *= 2
    here = z * ns + s
    dma = lambda n: pltpu.SemaphoreType.DMA((n,))
    buf = lambda *dims: pltpu.VMEM(dims, BF)

    def to_role(x):
        return x

    def gather(x):
        return [x] + [flip(x, axes, j) for j in range(1, ns)]

    spans = span_info.shape[1]
    def whole(w, *others):
        w = tie(w, *others)
        return w, flip(w, "mp", 1)

    low0, payload = run(
        first_body, (shape((own, d), BF), shape((own + 2 * spans + 8, d), BF)),
        span_info, mask_vector, inputs, grad_output, grad_bounds, name="first", smem=1, hbm=4,
        scratch=(pltpu.VMEM((own, d), F32), pltpu.VMEM((1, d), F32), pltpu.VMEM((own, d), F32), pltpu.VMEM((spans, 2, d), F32), dma(4)),
    )
    wk, wv, wq = whole(w_key), whole(w_value), whole(w_query)
    small_bufs = (shape((d, hw), BF),) * 6
    low0, *bufs = run(
        load_body, (shape((own, d), BF),) + small_bufs, to_role(low0), *wk, *wv, *wq, name="load", hbm=6, scratch=(dma(6),)
    )
    bkv, bq = bufs[:4], bufs[4:]
    parts = gather(low0)
    wi, wu = whole(w_inner, low0), whole(w_outer, low0)
    wo = whole(w_output, parts[1])
    payload = to_role(payload)

    per = d // (ns * nd)
    base = jnp.concatenate([(here ^ r) * per + jnp.arange(per, dtype=I32) for r in order_of(masks)])
    sel = (base[:, None] == jnp.arange(d, dtype=I32)[None, :]).astype(BF)
    picks = sel.shape[0]
    gains, biases = norm_gain.transpose(0, 2, 1), norm_bias.transpose(0, 2, 1)

    full = shape((tok, d))
    full_low = shape((tok, d), BF)
    column = shape((tok, 1))
    wide = shape((tok, 2 * f), BF)
    kv_shape = shape((tok, 4 * hw), BF)
    prob_shape = shape((heads, 2 * tok, tok), BF)
    piece = (shape((picks, f)), shape((picks, f), BF))
    two = shape((2, d))
    weight_bufs = (shape((d, hw), BF),) * 2 + (shape((d, f), BF),) * 4

    def other(*xs):
        return [flip(x, "mp", 1) for x in xs]

    hid, low, k, v = run(kv_first_body, (full, full_low, full_low, full_low), *parts, *bkv, name="keys_first", us=1, after=(sel, payload))
    ko, vo = other(k, v)
    (q,) = run(q_body, (full_low,), low, *bq, name="queries", us=0.6)
    payloads = gather(payload)
    probs, mixed, n1, r1, ln, act, dgelu, n2, r2, hid, low1, k1, v1, *bufs = run(
        forward_body,
        (prob_shape, full_low, full, column, full_low, wide, wide, full, column, full, full_low, full_low, full_low) + weight_bufs + small_bufs,
        q, k, v, ko, vo, hid, gains, biases, *wo, *wi, *wu, *wk, *wv, *wq,
        name="forward", hbm=12, scratch=(dma(12),), us=8,
    )
    bufs0, bkv, bq = bufs[:6], bufs[6:10], bufs[10:]
    k1o, v1o = other(k1, v1)
    (q1,) = run(q_body, (full_low,), low1, *bq, name="queries", us=0.6, after=payloads[1:])
    grad, marks = run(top_body, (full, shape((tok, LANES))), *payloads, name="top", us=TOP)
    probs1, mixed1, n11, r11, ln1, dgelu1, hid, mid, lmid, vec2, keep, send, *bufs1 = run(
        turn_body,
        (prob_shape, full_low, full, column, full_low, wide, full, full, full_low, two) + piece + weight_bufs,
        q1, k1, v1, k1o, v1o, hid, gains, biases, grad, sel, *wo, *wi, *wu,
        name="turn", hbm=6, scratch=(buf(tok, 2 * f), dma(6)), us=8,
    )

    def join(pairs, after=()):
        width = sum(k.shape[1] for k, _ in pairs)
        n = picks // 2
        return run(
            join_body(len(pairs)), (shape((n, width)), shape((n, width), BF)),
            *[k for k, _ in pairs], *[g for _, g in pairs], name="join", after=after,
        )

    def send_on(pair, step):
        return pair[0], flip(pair[1], axes, masks[step])

    def add(pair, after=()):
        keep, got = pair
        n, w = keep.shape[0] // 2, keep.shape[1]
        if n % 16:
            total = keep + got.astype(F32)
            return total[:n], total[n:].astype(BF)
        return run(add_body, (shape((n, w)), shape((n, w), BF)), keep, got, name="add", after=after)

    def rest(pair):
        for i in range(2, len(masks)):
            pair = send_on(add(pair), i)
        return pair

    def halves(keep, send):
        return keep, flip(send, "mp", 1)

    def ffn_back(layer, bufs, mid, lmid, dgelu, n1, r1, after=()):
        return run(
            ffn_back_body(layer), (wide, full, full_low, full_low, two),
            mid, lmid, dgelu, gains, n1, r1, *bufs, name="ffn_back", us=3.8, after=after,
        )

    def attend_back(mix, mixed, probs, q, v, vo, after=()):
        return run(
            attend_back_body, (prob_shape, full_low, full_low), mix, mixed, probs, q, v, vo, name="attend_back", us=2.3, after=after
        )

    def grad_pair(a, b, after=(), name=None, us=0.9):
        w = b.shape[1] // 2
        return run(grad_one_body, (shape((picks, w)), shape((picks, w), BF)), sel, a, b, name=name, us=us, after=after)

    outer1 = halves(keep, send)
    inner, res, lres1, mix, vec1 = ffn_back(1, bufs1, mid, lmid, dgelu1, n11, r11)
    inner1 = halves(*grad_pair(ln1, inner, name="grad_inner"))
    dscores, *dkv2 = attend_back(mix, mixed1, probs1, q1, v1, v1o, after=(inner1[0],))
    dkv2 = other(*dkv2)
    ffn1 = join([outer1, inner1], after=(dscores,))
    dk, dv, gq, part = run(
        attend_back_own, (full, full, full_low, full), mix, probs1, dscores, q1, k1, k1o, res, *bq,
        name="attend_back_own", us=2, after=(ffn1[0],),
    )
    ffn1 = send_on(ffn1, 0)
    gk, gv, mid, lmid, vec02, keep, send = run(
        next_layer_body, (full_low, full_low, full, full_low, two) + piece,
        part, dk, dv, *dkv2, *bkv, n2, r2, gains, sel, act, name="next_layer", us=2.5,
    )
    outer0 = halves(keep, send)
    attn = (shape((picks, 4 * hw)), shape((picks, 4 * hw), BF))
    att1 = halves(*run(grad_attention_body, attn, sel, lres1, mixed1, low1, gq, gk, gv, name="grad_attention", after=(mid,)))
    inner, res, lres0, mix, vec01 = ffn_back(0, bufs0, mid, lmid, dgelu, n1, r1, after=(att1[0],))
    inner0 = halves(*grad_pair(ln, inner, name="grad_inner"))
    dscores, *dkv2 = attend_back(mix, mixed, probs, q, v, vo, after=(inner0[0],))
    dkv2 = other(*dkv2)
    ffn1 = add(ffn1, after=(dscores,))
    att1 = join([att1], after=(ffn1[0],))
    ffn1 = send_on(ffn1, 1)
    ffn0 = join([outer0, inner0], after=(att1[0],))
    att1 = send_on(att1, 0)
    (res_out,) = run(result_body, (shape((own + 2 * spans, d)),), hid, payloads[0], name="result", after=(ffn0[0],))
    wo0 = halves(*grad_pair(lres0, mixed, name="grad_output", after=(res_out,)))
    dk, dv, gq, part, *bufs = run(
        attend_back_load_body, (full, full, full_low, full) + small_bufs, mix, probs, dscores, q, k, ko, res, *wq, *wk, *wv,
        name="attend_back_own", us=2, after=(wo0[0],), hbm=6, scratch=(dma(6),),
    )
    ffn0 = send_on(ffn0, 0)
    attn = (shape((picks, 3 * hw + LANES)), shape((picks, 3 * hw + LANES), BF))
    grad_in, keep, send = run(
        last_body, (shape((own, d)),) + attn, part, dk, dv, *dkv2, *bufs[:4], sel, low, gq, marks, vec01, vec02, vec1, vec2,
        name="last", scratch=(buf(tok, 2 * hw), buf(tok, 2 * hw)), us=2.5,
    )
    att0 = halves(keep, send)
    att1 = add(att1, after=(keep,))
    ffn0 = add(ffn0, after=(att1[0], ffn1[1]))
    att1 = send_on(att1, 1)
    att0 = join([att0, wo0], after=(ffn0[0],))
    ffn0 = send_on(ffn0, 1)
    att0 = add(send_on(att0, 0), after=(att1[1],))
    att0 = send_on(att0, 1)
    ffn1, att1, ffn0, att0 = [rest(x) for x in (ffn1, att1, ffn0, att0)]
    grad_in = to_role(grad_in)
    (grad_inputs,) = run(
        place_body, (shape((1, t, d)),), grad_in, flip(grad_in, "mp", 1), name="grad_inputs", scratch=(dma(2),), out_specs=(HB,)
    )
    res_out = to_role(res_out)
    outputs, bound_rows = run(
        put_body, (shape((1, t, d)), shape((1, spans, 2, d))), res_out, flip(res_out, "mp", 1),
        name="put", scratch=(pltpu.VMEM((spans, 2, d), F32), dma(3)), out_specs=(HB, HB),
    )

    def finish(pairs, count, width, places=None, extra=(), name=None):
        outs = (shape((LAYERS, per, width)),) * count + tuple(extra)
        places = places or [(j * width, j * width) for j in range(count)]
        return pl.pallas_call(
            finish_body(places, width, len(pairs[0])), out_shape=outs,
            compiler_params=pltpu.CompilerParams(vmem_limit_bytes=LIMIT), name=name,
        )(*pairs[0], *pairs[1])

    g_outer, g_inner = finish((ffn0, ffn1), 2, f, name="finish_ffn")
    vec_shape = shape((LAYERS, per, 2))
    places = [(i * hw, (i + 1) * hw) for i in range(3)] + [(3 * hw + LANES, 0)]
    g_query, g_key, g_value, g_output, g_gain, g_bias, g_mask = finish(
        (att0, att1), 4, hw, places, (vec_shape, vec_shape, shape((1, per))), name="finish_attention"
    )
    return outputs, bound_rows, grad_inputs, g_mask, g_query, g_key, g_value, g_output, g_inner, g_outer, g_gain, g_bias


def solution(mesh):
    row = P("dp", "seq", None)
    wide = P(None, None, "mp")
    out_w = P(None, ("dp", "seq"), "mp")
    out_v = P(None, ("dp", "seq"), None)
    return jax.shard_map(
        on_device,
        mesh=mesh,
        in_specs=(row, row, P(), wide, wide, wide, wide, wide, wide, P(), P(), row, P("dp", "seq", None, None)),
        out_specs=(row, P("dp", "seq", None, None), row, P(None, ("dp", "seq"))) + (out_w,) * 6 + (out_v,) * 2,
        check_vma=False,
    )
```

```python
import jax
import jax.numpy as jnp
from jax import lax
from jax.experimental import pallas as pl
from jax.experimental.pallas import tpu as pltpu
from jax.sharding import PartitionSpec as P

HD = 64
LAYERS = 2
EPS = 1e-12
SCALE = HD**-0.5
BF = jnp.bfloat16
F32 = jnp.float32
I32 = jnp.int32
LANES = 128
LIMIT = 3 * 2**20
BIG = 6 * 2**20
FORWARD = 15 * 2**20
RATE = 0.3e9
LONG = 8
GROUP = 6
VM = pl.BlockSpec(memory_space=pltpu.VMEM)
SM = pl.BlockSpec(memory_space=pltpu.SMEM)
HB = pl.BlockSpec(memory_space=pltpu.HBM)
ANY = pl.BlockSpec(memory_space=pl.ANY)


def shape(dims, kind=F32):
    return jax.ShapeDtypeStruct(tuple(dims), kind)


def run(body, outs, *args, name=None, smem=0, hbm=0, free=0, scratch=(), out_specs=None, limit=LIMIT, us=1.0, after=()):
    hbm_end = len(args) - free
    specs = [SM] * smem + [VM] * (hbm_end - smem - hbm) + [HB] * hbm + [ANY] * free + [pl.BlockSpec(memory_space=pl.ANY)] * len(after)
    count = len(args)
    held = tuple(pltpu.with_memory_space_constraint(a, pltpu.HBM) for a in args[hbm_end - hbm : hbm_end])
    args = args[: hbm_end - hbm] + held + args[hbm_end:]
    def whole(*refs):
        body(*refs[:count], *refs[count + len(after) :])

    return pl.pallas_call(
        whole,
        out_shape=tuple(outs),
        in_specs=specs,
        out_specs=(VM,) * len(outs) if out_specs is None else tuple(out_specs),
        scratch_shapes=scratch,
        compiler_params=pltpu.CompilerParams(vmem_limit_bytes=limit),
        cost_estimate=pl.CostEstimate(flops=int(us * RATE), bytes_accessed=1, transcendentals=0),
        name=name,
    )(*args, *after)


def dot(a, b, ca, cb):
    return lax.dot_general(a, b, (((ca,), (cb,)), ((), ())), preferred_element_type=F32)


def flip(x, axis, mask):
    count = lax.axis_size(axis)
    return lax.ppermute(x, axis, [(i, i ^ mask) for i in range(count)])


KEY, VALUE, QUERY, OUT = range(4)


def sides(own, other, n):
    return own.at[n], other.at[n]


def own_place(own):
    return lax.axis_index("seq") * (2 * own) + lax.axis_index("mp") * own


def load(layer, weights, packed, sems, first=0):
    copies = [pltpu.make_async_copy(w.at[layer], packed.at[i], sems.at[first + i]) for i, w in enumerate(weights)]
    for c in copies:
        c.start()
    return copies


def start_body(spans, mask_vector, inputs, grads, bounds, wk, wv, wq, wo, packet, attention, hid, mv, gv, bv, sems, wsems):
    own, d = hid.shape
    n = spans.shape[1]
    at = lax.axis_index("mp") * own
    copies = [
        pltpu.make_async_copy(inputs.at[0, pl.ds(at, own)], hid, sems.at[0]),
        pltpu.make_async_copy(mask_vector, mv.at[0], sems.at[1]),
        pltpu.make_async_copy(grads.at[0, pl.ds(at, own)], gv, sems.at[2]),
        pltpu.make_async_copy(bounds.at[0], bv, sems.at[3]),
    ]
    for c in copies:
        c.start()
    weights = load(0, (wk, wv, wq, wo), attention, wsems)
    pos = lax.broadcasted_iota(I32, (own, 1), 0) + own_place(own)
    lane = lax.broadcasted_iota(I32, (8, d), 1) % (2 * n)
    mask = pos < 0
    edges = jnp.zeros((8, d), I32)
    for i in range(n):
        a, e = spans[0, i, 0], spans[0, i, 0] + spans[0, i, 1]
        mask = mask | ((pos >= a) & (pos < e))
        edges = jnp.where(lane == 2 * i, a - 1, jnp.where(lane == 2 * i + 1, e, edges))
    upper = lax.broadcasted_iota(I32, (8, d), 0) < 4
    edges = jnp.where(upper, edges // 16, edges % 16).astype(F32)
    copies[0].wait()
    copies[1].wait()
    x = jnp.where(mask, mv[...], hid[...])
    packet[0:own] = x.astype(BF)
    copies[2].wait()
    copies[3].wait()
    packet[own : 2 * own] = gv[...].astype(BF)
    packet[2 * own :] = jnp.concatenate([bv[i] for i in range(n)] + [edges], axis=0).astype(BF)
    for c in weights:
        c.wait()


def load_body(wk, wv, wq, wo, wi, wu, attention, wi0, wu0, wi1, wu1, sems):
    copies = load(1, (wk, wv, wq, wo), attention, sems)
    for i, (w, layer, b) in enumerate(((wi, 0, wi0), (wu, 0, wu0), (wi, 1, wi1), (wu, 1, wu1))):
        copies.append(pltpu.make_async_copy(w.at[layer], b, sems.at[4 + i]))
        copies[-1].start()
    for c in copies:
        c.wait()


def kv_first_body(*refs):
    parts, (am, other, hid, low, k, v, ao, sems) = refs[:-8], refs[-8:]
    copies = [pltpu.make_async_copy(other.at[i], ao.at[i], sems.at[i]) for i in range(4)]
    for c in copies:
        c.start()
    r = hid.shape[0] // len(parts)
    for i, p in enumerate(parts):
        sl = slice(i * r, (i + 1) * r)
        hid[sl] = p[0:r].astype(F32)
        low[sl] = p[0:r]
    copies[KEY].wait()
    copies[VALUE].wait()
    kv_body(low, am, ao, k, v)
    copies[QUERY].wait()
    copies[OUT].wait()


def kv_body(low, am, ao, k, v):
    x = low[...]
    for out, n in ((k, KEY), (v, VALUE)):
        h = out.shape[1] // 2
        for i, w in enumerate(sides(am, ao, n)):
            out[:, i * h : (i + 1) * h] = dot(x, w[...], 1, 0).astype(BF)


def q_body(low, am, ao, q):
    h = q.shape[1] // 2
    x = low[...]
    for i, w in enumerate(sides(am, ao, QUERY)):
        q[:, i * h : (i + 1) * h] = (dot(x, w[...], 1, 0) * SCALE).astype(BF)


def halves_of_pair():
    lanes = lax.broadcasted_iota(I32, (1, LANES), 1) < HD
    rows = lax.broadcasted_iota(I32, (LANES, 1), 0) < HD
    return lanes, rows


def rows_of(own, oth, g):
    pairs = own.shape[1] // LANES
    g2 = (g + pairs // 2) % pairs
    return jnp.concatenate([own[:, g * LANES : (g + 1) * LANES], oth[:, g2 * LANES : (g2 + 1) * LANES]], axis=0)


def normalize(a):
    mu = jnp.mean(a, axis=-1, keepdims=True)
    sh = a - mu
    rstd = lax.rsqrt(jnp.mean(sh * sh, axis=-1, keepdims=True) + EPS)
    return sh * rstd, rstd


def attend(q, k, v, ko, vo, probs, mixed):
    width = q.shape[1]
    pairs = width // LANES
    lo, top = halves_of_pair()
    for g0 in range(0, pairs, GROUP):
        scores = []
        for g in range(g0, g0 + GROUP):
            qq = q[:, g * LANES : (g + 1) * LANES]
            kk = rows_of(k, ko, g)
            scores += [dot(kk, jnp.where(m, qq, 0), 1, 1) for m in (lo, ~lo)]
        exps = [jnp.exp(s - jnp.max(s, axis=0, keepdims=True)) for s in scores]
        low = [(e * (1.0 / jnp.sum(e, axis=0, keepdims=True))).astype(BF) for e in exps]
        for j in range(2 * GROUP):
            probs[2 * g0 + j] = low[j]
        for g in range(g0, g0 + GROUP):
            j = 2 * (g - g0)
            vv = rows_of(v, vo, g)
            r = jnp.where(top, dot(vv, low[j], 0, 0), dot(vv, low[j + 1], 0, 0))
            mixed[:, g * LANES : (g + 1) * LANES] = r.T.astype(BF)


def attend_out(hid, mixed, am, ao, gain, bias, n1, r1, ln):
    h = mixed.shape[1] // 2
    branch = None
    for i, w in enumerate(sides(am, ao, OUT)):
        y = dot(mixed[:, i * h : (i + 1) * h], w[...], 1, 1)
        branch = y if branch is None else branch + y
    n, r = normalize(hid[...] + branch)
    n1[...] = n
    r1[...] = r
    y = n * gain + bias
    ln[...] = y.astype(BF)
    return y


def ffn_half(x, i, wi, wu, act, dgelu):
    f = wi.shape[1]
    inner = dot(x, wi[...], 1, 0)
    cdf = 0.5 + 0.5 * lax.erf(inner * 0.7071067811865476)
    a = (inner * cdf).astype(BF)
    act[:, i * f : (i + 1) * f] = a
    dgelu[:, i * f : (i + 1) * f] = (cdf + inner * jnp.exp(-0.5 * inner * inner) * 0.3989422804014327).astype(BF)
    return dot(a, wu[...], 1, 1)


def norm_back(grad, n, rstd, gain):
    e = grad * gain
    back = (e - jnp.mean(e, axis=-1, keepdims=True) - n * jnp.mean(e * n, axis=-1, keepdims=True)) * rstd
    return back, jnp.sum(grad * n, axis=0, keepdims=True), jnp.sum(grad, axis=0, keepdims=True)


def weight_grad(sel, a, bs, keep, send, at=0):
    pick = dot(sel[...], a[...], 1, 1).astype(BF)
    for b in bs:
        h = b.shape[1] // 2
        keep[:, at : at + h] = dot(pick, b[:, :h], 1, 0)
        send[:, at : at + h] = dot(pick, b[:, h:], 1, 0).astype(BF)
        at += h


def attend_layer_body(layer):
    def body(q, k, v, ko, vo, hid, gains, biases, am, ao, probs, mixed, n1, r1, ln, y):
        attend(q, k, v, ko, vo, probs, mixed)
        y[...] = attend_out(hid, mixed, am, ao, gains[layer, 0:1], biases[layer, 0:1], n1, r1, ln)

    return body


def ffn_part_body(ln, wi, wu, act, dgelu, out):
    out[...] = ffn_half(ln[...], 0, wi, wu, act, dgelu).astype(out.dtype)


def ffn_end_body(y, part, got, gains, biases, am, ao, n2, r2, hid, low, k, v):
    n, r = normalize(y[...] + part[...] + got[...].astype(F32))
    n2[...] = n
    r2[...] = r
    x = n * gains[0, 1:2] + biases[0, 1:2]
    hid[...] = x
    low[...] = x.astype(BF)
    kv_body(low, am, ao, k, v)


def turn_body(y, part, got, gains, biases, grad, hid, mid, lmid, la, lb, vec):
    n, r = normalize(y[...] + part[...] + got[...].astype(F32))
    hid[...] = n * gains[1, 1:2] + biases[1, 1:2]
    middle_back(grad[...], n, r, gains[1, 1:2], mid, lmid, (la, lb), vec)


def rows_joined(pieces):
    return jnp.concatenate([p[...] for p in pieces], axis=0)


def store_rows(x, pieces):
    n = pieces[0].shape[0]
    for i, p in enumerate(pieces):
        p[...] = x[i * n : (i + 1) * n].astype(p.dtype)


def middle_back(grad, n, r, gain, mid, lmid, pieces, vec):
    back, gg, gb = norm_back(grad, n, r, gain)
    mid[...] = back
    lmid[...] = back.astype(BF)
    store_rows(back, pieces)
    vec[0:1] = gg
    vec[1:2] = gb


def ffn_back_own_body(lmid, dgelu, wi, wu, inner, out):
    g = (dot(lmid[...], wu[...], 1, 0) * dgelu[...].astype(F32)).astype(BF)
    inner[...] = g
    out[...] = dot(g, wi[...], 1, 1)


def ffn_back_other_body(la, lb, dgelu, wi, wu, inner, oa, ob):
    g = (dot(rows_joined((la, lb)), wu[...], 1, 0) * dgelu[...].astype(F32)).astype(BF)
    inner[...] = g
    store_rows(dot(g, wi[...], 1, 1), (oa, ob))


def weight_feed_body(sel, lmid, la, lb, ln, lno, act, acto, inner, innero, rest, send):
    n, f = rest.shape[0], act.shape[1]
    for i, (a, ao, b, bo) in enumerate(((lmid[...], rows_joined((la, lb)), act, acto), (ln[...], lno[...], inner, innero))):
        pick = dot(sel[...], a, 1, 1).astype(BF)
        picko = dot(sel[...], ao, 1, 1).astype(BF)
        g = dot(pick, b[...], 1, 0) + dot(picko, bo[...], 1, 0)
        rest[:, i * f : (i + 1) * f] = g[0:n]
        send[:, i * f : (i + 1) * f] = g[n:].astype(BF)


def ffn_back_end_body(layer):
    def body(mid, part, ga, gb, gains, n1, r1, am, ao, res, lres, mix, vec):
        total = mid[...] + part[...] + rows_joined((ga, gb)).astype(F32)
        back, gain_sum, bias_sum = norm_back(total, n1[...], r1[...], gains[layer, 0:1])
        res[...] = back
        low = back.astype(BF)
        lres[...] = low
        vec[0:1] = gain_sum
        vec[1:2] = bias_sum
        h = mix.shape[1] // 2
        for i, w in enumerate(sides(am, ao, OUT)):
            mix[:, i * h : (i + 1) * h] = dot(low, w[...], 1, 0).astype(BF)

    return body


def load_beside(body, count):
    def both(*refs):
        sources, attention, sems = refs[count : count + 4], refs[-2], refs[-1]
        copies = [pltpu.make_async_copy(w.at[0], attention.at[i], sems.at[i]) for i, w in enumerate(sources)]
        for c in copies:
            c.start()
        body(*refs[:count], *refs[count + 4 : -2])
        for c in copies:
            c.wait()

    return both


def load_other_beside(body, count):
    def both(*refs):
        source, attention, sems = refs[count], refs[-2], refs[-1]
        copies = [pltpu.make_async_copy(source.at[i], attention.at[i], sems.at[i]) for i in range(4)]
        for c in copies:
            c.start()
        body(*refs[:count], *refs[count + 1 : -2])
        for c in copies:
            c.wait()

    return both


def grad_one_body(sel, a, b, keep, send):
    weight_grad(sel, a, (b,), keep, send)


def grad_two_body(sel, a, b, c, d, keep, send):
    weight_grad(sel, a, (b,), keep, send)
    weight_grad(sel, c, (d,), keep, send, b.shape[1] // 2)


def attend_back_body(mix, mixed, probs, q, v, vo, dscores, *theirs):
    t, width = q.shape
    pairs = width // LANES
    lo, top = halves_of_pair()
    for g in range(pairs):
        sl = slice(g * LANES, (g + 1) * LANES)
        gg = mix[:, sl]
        vv = rows_of(v, vo, g)
        delta = (gg.astype(F32) * mixed[:, sl].astype(F32)).T
        ds = []
        for j, m in enumerate((lo, ~lo)):
            dl = jnp.sum(delta[j * HD : (j + 1) * HD], axis=0, keepdims=True)
            dp = dot(vv, jnp.where(m, gg, 0), 1, 1)
            ds.append((probs[2 * g + j].astype(F32) * (dp - dl)).astype(BF))
            dscores[2 * g + j] = ds[j]
        qq = q[:, sl]
        at = (g + pairs // 2) % pairs * LANES
        count = len(theirs) // 2
        dk, dv = theirs[at * count // width], theirs[count + at * count // width]
        at = at % (width // count)
        to = slice(at, at + LANES)
        dk[:, to] = jnp.where(lo, dot(ds[0][t:], qq, 1, 0), dot(ds[1][t:], qq, 1, 0)).astype(BF)
        dv[:, to] = jnp.where(lo, dot(probs[2 * g, t:], gg, 1, 0), dot(probs[2 * g + 1, t:], gg, 1, 0)).astype(BF)


def attend_back_own(mix, probs, dscores, q, k, ko, res, am, ao, dk, dv, gq, rest):
    t, width = q.shape
    pairs = width // LANES
    lo, top = halves_of_pair()
    for g in range(pairs):
        sl = slice(g * LANES, (g + 1) * LANES)
        gg, qq = mix[:, sl], q[:, sl]
        kk = rows_of(k, ko, g)
        dq = jnp.where(top, dot(kk, dscores[2 * g], 0, 0), dot(kk, dscores[2 * g + 1], 0, 0))
        gq[:, sl] = (dq * SCALE).T.astype(BF)
        dk[:, sl] = jnp.where(lo, dot(dscores[2 * g, :t], qq, 1, 0), dot(dscores[2 * g + 1, :t], qq, 1, 0))
        dv[:, sl] = jnp.where(lo, dot(probs[2 * g, :t], gg, 1, 0), dot(probs[2 * g + 1, :t], gg, 1, 0))
    h = width // 2
    total = res[...]
    for i, w in enumerate(sides(am, ao, QUERY)):
        total = total + dot(gq[:, i * h : (i + 1) * h], w[...], 1, 1)
    rest[...] = total


def hidden_back(rest, dk, dv, ka, kb, va, vb, am, ao, gk, gv):
    total = rest[...]
    for own, theirs, out, n in ((dk, (ka, kb), gk, KEY), (dv, (va, vb), gv, VALUE)):
        h = out.shape[1] // 2
        for i, w in enumerate(sides(am, ao, n)):
            sl = slice(i * h, (i + 1) * h)
            g = (own[:, sl] + theirs[i][...].astype(F32)).astype(BF)
            out[:, sl] = g
            total = total + dot(g, w[...], 1, 1)
    return total


def next_layer_body(rest, dk, dv, ka, kb, va, vb, am, ao, n2, r2, gains, gk, gv, mid, lmid, la, lb, vec):
    grad = hidden_back(rest, dk, dv, ka, kb, va, vb, am, ao, gk, gv)
    middle_back(grad, n2[...], r2[...], gains[0, 1:2], mid, lmid, (la, lb), vec)


def grad_attention_body(sel, lres, mixed, low, gq, gk, gv, keep, send, keep2, send2):
    weight_grad(sel, lres, (mixed,), keep, send)
    weight_grad(sel, low, (gq,), keep, send, mixed.shape[1] // 2)
    weight_grad(sel, low, (gk, gv), keep2, send2)


def split_dot(onehot, x, ca, cb):
    total = None
    for _ in range(3):
        part = x.astype(BF)
        x = x - part.astype(F32)
        y = dot(onehot, part, ca, cb)
        total = y if total is None else total + y
    return total


def last_body(rest, dk, dv, dk2, dv2, am, ao, sel, low, marks, v1, v2, v3, v4, grad_in, keep, send, gk, gv):
    w = gk.shape[1]
    own, h = grad_in.shape[0], w // 2
    grad = hidden_back(rest, dk, dv, dk2[:, :h], dk2[:, h:], dv2[:, :h], dv2[:, h:], am, ao, gk, gv)
    weight_grad(sel, low, (gk, gv), keep, send)
    grad_in[...] = jnp.where(marks[0:own, 0:1] > 0.5, 0.0, grad[0:own])
    mask = jnp.sum(grad * marks[:, 0:1], axis=0, keepdims=True)
    rows = jnp.concatenate([v1[...], v2[...], v3[...], v4[...], jnp.broadcast_to(mask, (8,) + mask.shape[1:])], axis=0)
    rows = jnp.concatenate([rows, jnp.zeros((LANES - rows.shape[0], rows.shape[1]), F32)], axis=0)
    small = split_dot(sel[...], rows, 1, 1)
    keep[:, w:] = small
    send[:, w:] = small.astype(BF)


def join_body(parts):
    def body(*refs):
        keeps, gots, rest, sends = refs[:parts], refs[parts : 2 * parts], refs[2 * parts], refs[2 * parts + 1 :]
        n, at = rest.shape[0], 0
        for keep, got in zip(keeps, gots):
            to = slice(at, at + keep.shape[1])
            rest[:, to] = keep[0:n] + got[0:n].astype(F32)
            for i, x in enumerate(sends):
                sl = slice((i + 1) * n, (i + 2) * n)
                x[:, to] = (keep[sl] + got[sl].astype(F32)).astype(BF)
            at += keep.shape[1]

    return body


def add_body(keep, got, rest, send):
    n = rest.shape[0]
    rest[...] = keep[0:n] + got[0:n].astype(F32)
    send[...] = (keep[n:] + got[n:].astype(F32)).astype(BF)


def top_body(*refs):
    n = len(refs) - 2
    parts, (grad, marks) = refs[:n], refs[n:]
    h = grad.shape[0] // n
    lane = lax.broadcasted_iota(I32, (1, LANES), 1)
    edges = jnp.full((1, LANES), -8.0, F32)
    bounds = []
    for j, p in enumerate(parts):
        tail = p[2 * h :].astype(F32)
        b = tail.shape[0] - 8
        edges = jnp.where((lane >= j * b) & (lane < (j + 1) * b), edges_of(tail), edges)
        bounds.append(tail[0:b])
    bounds = jnp.concatenate(bounds, axis=0)
    bounds = jnp.concatenate([bounds, jnp.zeros((LANES - bounds.shape[0], bounds.shape[1]), F32)], axis=0).astype(BF)
    row = lax.broadcasted_iota(I32, (h, 1), 0)
    even = (lane % 2) == 0
    for j, p in enumerate(parts):
        pos = (row + block_place(j, h)).astype(F32)
        onehot = jnp.where(pos == edges, 1.0, 0.0).astype(BF)
        grad[j * h : (j + 1) * h] = p[h : 2 * h].astype(F32) + dot(onehot, bounds, 1, 0)
        after = jnp.where((even & (pos > edges)) & (edges > -4.0), 1.0, 0.0) - jnp.where((~even & (pos >= edges)) & (edges > -4.0), 1.0, 0.0)
        marks[j * h : (j + 1) * h] = jnp.broadcast_to(jnp.sum(after, axis=1, keepdims=True), (h, LANES))


def block_place(j, own):
    return (lax.axis_index("seq") ^ j) * (2 * own) + lax.axis_index("mp") * own


def edges_of(payload):
    e = payload[-8:, 0:LANES].astype(F32)
    return e[0:1] * 16.0 + e[4:5]


def result_body(hid, payload, out):
    own = hid.shape[0] // lax.axis_size("seq")
    n = out.shape[0] - own
    out[0:own] = hid[0:own]
    row = jnp.broadcast_to(edges_of(payload), (8, LANES)).T[0:n, 0:1]
    lane = lax.broadcasted_iota(I32, (1, own), 1)
    total = None
    for j in range(hid.shape[0] // own):
        pos = (lane + block_place(j, own)).astype(F32)
        onehot = jnp.where(row == pos, 1.0, 0.0).astype(BF)
        y = split_dot(onehot, hid[j * own : (j + 1) * own], 1, 0)
        total = y if total is None else total + y
    out[own:] = total


def put_body(mine, other, out, bound, rows, sems):
    n = bound.shape[1] * 2
    own = mine.shape[0] - n
    m = lax.axis_index("mp")
    a = pltpu.make_async_copy(mine.at[0:own], out.at[0, pl.ds(m * own, own)], sems.at[0])
    b = pltpu.make_async_copy(other.at[0:own], out.at[0, pl.ds((1 - m) * own, own)], sems.at[1])
    a.start()
    b.start()
    total = mine[own:] + other[own:]
    for i in range(n // 2):
        rows[i] = total[2 * i : 2 * i + 2]
    c = pltpu.make_async_copy(rows, bound.at[0], sems.at[2])
    c.start()
    a.wait()
    b.wait()
    c.wait()


def place_body(mine, other, out, sems):
    own = mine.shape[0]
    m = lax.axis_index("mp")
    a = pltpu.make_async_copy(mine, out.at[0, pl.ds(m * own, own)], sems.at[0])
    b = pltpu.make_async_copy(other, out.at[0, pl.ds((1 - m) * own, own)], sems.at[1])
    a.start()
    b.start()
    a.wait()
    b.wait()


def finish_body(places, width, terms):
    def body(*refs):
        layers, outs = (refs[: terms[0]], refs[terms[0] : sum(terms)]), refs[sum(terms) :]

        def total(i, sl):
            x = layers[i][0][:, sl]
            for r in layers[i][1:]:
                x = x + r[:, sl].astype(F32)
            return x

        for i in range(LAYERS):
            for j, at in enumerate(places):
                outs[j][i] = total(i, slice(at[i], at[i] + width))
        if len(outs) > len(places):
            gain, bias, mask = outs[len(places) :]
            small = total(0, slice(4 * width, 4 * width + LANES)).T
            for i in range(LAYERS):
                for j in range(2):
                    at = 4 * i + 2 * j
                    gain[i, j : j + 1] = small[at : at + 1]
                    bias[i, j : j + 1] = small[at + 1 : at + 2]
            mask[...] = small[8:9]

    return body


def order_of(masks):
    if not masks:
        return [0]
    rest = order_of(masks[1:])
    return rest + [r ^ masks[0] for r in rest]


def tie(x, *others):
    return lax.optimization_barrier((x,) + others)[0]


def on_device(inputs, span_info, mask_vector, w_query, w_key, w_value, w_output, w_inner, w_outer, norm_gain, norm_bias, grad_output, grad_bounds):
    t, d = inputs.shape[1:]
    ns, nd = lax.axis_size("seq"), lax.axis_size("dp")
    s, z = lax.axis_index("seq"), lax.axis_index("dp")
    f = w_inner.shape[2]
    hw = w_query.shape[2]
    heads = 2 * hw // HD
    own = t // 2
    tok = own * ns
    axes = ("dp", "seq")
    masks = []
    bit = ns
    while bit < ns * nd:
        masks.append(bit)
        bit *= 2
    here = z * ns + s
    dma = lambda n: pltpu.SemaphoreType.DMA((n,))
    buf = lambda *dims: pltpu.VMEM(dims, BF)

    def to_role(x):
        return x

    def gather(x):
        return [x] + [flip(x, axes, j) for j in range(1, ns)]

    spans = span_info.shape[1]
    def other(*xs):
        return [flip(x, "mp", 1) for x in xs]

    weights = (w_key, w_value, w_query, w_output)
    attention = shape((4, d, hw), BF)
    packet, am0 = run(
        start_body, (shape((2 * own + 2 * spans + 8, d), BF), attention),
        span_info, mask_vector, inputs, grad_output, grad_bounds, *weights, name="start", smem=1, hbm=8,
        scratch=(pltpu.VMEM((own, d), F32), pltpu.VMEM((1, d), F32), pltpu.VMEM((own, d), F32), pltpu.VMEM((spans, 2, d), F32),
                 dma(4), dma(4)),
    )
    held0 = other(am0)[0]
    packets = gather(packet)
    feed_weight = shape((d, f), BF)
    am1, wi0, wu0, wi1, wu1 = run(
        load_body, (attention,) + (feed_weight,) * 4, *weights, w_inner, w_outer, name="load", hbm=6, scratch=(dma(8),), after=(packet,)
    )

    per = d // (ns * nd)
    base = jnp.concatenate([(here ^ r) * per + jnp.arange(per, dtype=I32) for r in order_of(masks)])
    sel = (base[:, None] == jnp.arange(d, dtype=I32)[None, :]).astype(BF)
    picks = sel.shape[0]
    gains, biases = norm_gain.transpose(0, 2, 1), norm_bias.transpose(0, 2, 1)

    full = shape((tok, d))
    full_low = shape((tok, d), BF)
    column = shape((tok, 1))
    wide = shape((tok, 2 * f), BF)
    kv_shape = shape((tok, 4 * hw), BF)
    prob_shape = shape((heads, 2 * tok, tok), BF)
    piece = (shape((picks, f)), shape((picks, f), BF))
    two = shape((2, d))

    hid, low, k, v, ao0 = run(
        kv_first_body, (full, full_low, full_low, full_low, attention), *packets, am0, held0,
        name="keys_first", hbm=1, scratch=(dma(4),), after=(sel, am1),
    )
    ko, vo = other(k, v)
    (q,) = run(q_body, (full_low,), low, am0, ao0, name="queries")
    ao1 = other(tie(am1, ko, vo))[0]
    narrow = shape((tok, f), BF)

    def attend_layer(layer, q, k, v, ko, vo, hid, am, ao):
        return run(
            attend_layer_body(layer), (prob_shape, full_low, full, column, full_low, full),
            q, k, v, ko, vo, hid, gains, biases, am, ao, name="attend", limit=BIG,
        )

    def ffn(ln, wi, wu):
        lno = other(ln)[0]
        act, dgelu, part = run(ffn_part_body, (narrow, narrow, full), ln, wi, wu, name="ffn_own")
        acto, dgeluo, parto = run(ffn_part_body, (narrow, narrow, full_low), lno, wi, wu, name="ffn_other", after=(part,))
        return lno, act, dgelu, acto, dgeluo, part, other(parto)[0]

    probs, mixed, n1, r1, ln, y = attend_layer(0, q, k, v, ko, vo, hid, am0, ao0)
    lno, act, dgelu, acto, dgeluo, part, got = ffn(ln, wi0, wu0)
    n2, r2, hid, low1, k1, v1 = run(
        ffn_end_body, (full, column, full, full_low, full_low, full_low), y, part, got, gains, biases, am1, ao1, name="ffn_end"
    )
    k1o, v1o = other(k1, v1)
    grad, marks = run(top_body, (full, shape((tok, LANES))), *packets, name="top", after=(k1,))
    (q1,) = run(q_body, (full_low,), low1, am1, ao1, name="queries", after=(grad,))
    probs1, mixed1, n11, r11, ln1, y = attend_layer(1, q1, k1, v1, k1o, v1o, hid, am1, ao1)
    ln1o, act1, dgelu1, act1o, dgelu1o, part, got = ffn(ln1, wi1, wu1)
    halved = (shape((tok // 2, d), BF),) * 2
    hid, mid, lmid, la, lb, vec2 = run(turn_body, (full, full, full_low) + halved + (two,), y, part, got, gains, biases, grad, name="turn")

    def join(pairs, blocks=2, after=()):
        width = sum(k.shape[1] for k, _ in pairs)
        n = picks // blocks
        return run(
            join_body(len(pairs)), (shape((n, width)),) + (shape((n, width), BF),) * (blocks - 1),
            *[k for k, _ in pairs], *[g for _, g in pairs], name="join", after=after,
        )

    def spread(pairs, after=()):
        if nd > 4:
            pair = send_on(join(pairs, after=after), 0)
            for i in range(1, len(masks)):
                pair = send_on(add(pair), i)
            return pair
        keep, *sends = join(pairs, nd, after=after)
        return [keep] + [flip(x, axes, o) for x, o in zip(sends, order_of(masks)[1:])]

    def send_on(pair, step):
        return pair[0], flip(pair[1], axes, masks[step])

    def add(pair, after=(), us=1.0):
        keep, got = pair
        n, w = keep.shape[0] // 2, keep.shape[1]
        if n % 16:
            total = keep + got.astype(F32)
            return total[:n], total[n:].astype(BF)
        return run(add_body, (shape((n, w)), shape((n, w), BF)), keep, got, name="add", after=after, us=us)

    def rest(pair):
        for i in range(2, len(masks)):
            pair = send_on(add(pair), i)
        return pair

    def halves(keep, send):
        return keep, flip(send, "mp", 1)

    group = (shape((picks // 2, 2 * f)), shape((picks // 2, 2 * f), BF))

    def ffn_back(layer, mid, lmid, lmids, dgelu, dgeluo, wi, wu, n1, r1, am, ao, after=(), between=None):
        lmids = other(*lmids)
        inner, part = run(ffn_back_own_body, (narrow, full), lmid, dgelu, wi, wu, name="ffn_back_own", after=after)
        innero, *parts = run(
            ffn_back_other_body, (narrow,) + halved, *lmids, dgeluo, wi, wu, name="ffn_back_other", after=(part,)
        )
        gots = other(*parts)
        ends = run(
            ffn_back_end_body(layer), (full, full_low, full_low, two), mid, part, *gots, gains, n1, r1, am, ao,
            name="ffn_back_end", after=between(lmids, inner, innero),
        )
        return (lmids, inner, innero) + tuple(ends)

    def grad_feed(lmid, lmids, ln, lno, act, acto, inner, innero, after=()):
        return run(weight_feed_body, group, sel, lmid, *lmids, ln, lno, act, acto, inner, innero, name="grad_feed", after=after)

    def attend_own(mix, probs, dscores, q, k, ko, res, am, ao, after=()):
        return run(
            attend_back_own, (full, full, full_low, full), mix, probs, dscores, q, k, ko, res, am, ao,
            name="attend_back_own", after=after,
        )

    def attend_back(mix, mixed, probs, q, v, vo, after=()):
        return run(
            attend_back_body, (prob_shape, shape((tok, 4 * hw), BF)), mix, mixed, probs, q, v, vo, name="attend_back", us=2.3, after=after
        )

    def grad_pair(a, b, after=(), name=None, us=0.9):
        w = b.shape[1] // 2
        return run(grad_one_body, (shape((picks, w)), shape((picks, w), BF)), sel, a, b, name=name, us=us, after=after)

    sums = {}

    def between(lmids, inner, innero):
        sums["ffn"] = grad_feed(lmid, lmids, ln1, ln1o, act1, act1o, inner, innero)
        return (sums["ffn"][0],)

    _, _, _, res, lres1, mix, vec1 = ffn_back(
        1, mid, lmid, (la, lb), dgelu1, dgelu1o, wi1, wu1, n11, r11, am1, ao1, between=between
    )
    ffn1 = send_on(sums["ffn"], 0)
    theirs = (shape((tok, hw), BF),) * 4
    dscores, *dkv2, am0 = run(
        load_beside(attend_back_body, 6), (prob_shape,) + theirs + (attention,), mix, mixed1, probs1, q1, v1, v1o, *weights,
        name="attend_back", hbm=4, scratch=(dma(4),),
    )
    dkv2 = other(*dkv2)
    dk, dv, gq, part_sum, ao0 = run(
        load_other_beside(attend_back_own, 9), (full, full, full_low, full, attention),
        mix, probs1, dscores, q1, k1, k1o, res, am1, ao1, held0, name="attend_back_own", hbm=1, scratch=(dma(4),),
    )
    gk, gv, mid, lmid, la, lb, vec02 = run(
        next_layer_body, (full_low, full_low, full, full_low) + halved + (two,), part_sum, dk, dv, *dkv2, am1, ao1, n2, r2, gains, name="next_layer"
    )
    attn = (shape((picks, 2 * hw)), shape((picks, 2 * hw), BF))
    keep, send, keep2, send2 = run(
        grad_attention_body, attn * 2, sel, lres1, mixed1, low1, gq, gk, gv, name="grad_attention", after=(mid,)
    )
    att1 = halves(keep, send), halves(keep2, send2)
    def between(lmids, inner, innero):
        sums["ffn"] = add(ffn1, after=(innero,))
        sums["attention"] = join(att1, after=(sums["ffn"][0],))
        return (sums["attention"][0],)

    lmids, inner, innero, res, lres0, mix, vec01 = ffn_back(
        0, mid, lmid, (la, lb), dgelu, dgeluo, wi0, wu0, n1, r1, am0, ao0, after=(keep,), between=between
    )
    att1 = send_on(sums["attention"], 0)
    dscores, *dkv2 = run(attend_back_body, (prob_shape, full_low, full_low), mix, mixed, probs, q, v, vo, name="attend_back")
    dkv2 = other(*dkv2)
    ffn0 = grad_feed(lmid, lmids, ln, lno, act, acto, inner, innero, after=(dscores,))
    ffn1 = send_on(sums["ffn"], 1)
    (res_out,) = run(result_body, (shape((own + 2 * spans, d)),), hid, packets[0], name="result", after=(ffn0[0], ffn1[0]))
    ffn0 = send_on(ffn0, 0)
    dk, dv, gq, part_sum = attend_own(mix, probs, dscores, q, k, ko, res, am0, ao0, after=(res_out,))
    query0 = halves(*run(
        grad_two_body, (shape((picks, 2 * hw)), shape((picks, 2 * hw), BF)), sel, lres0, mixed, low, gq, name="grad_query"
    ))
    att1 = add(att1, after=(query0[0],), us=LONG)
    attn = (shape((picks, 2 * hw + LANES)), shape((picks, 2 * hw + LANES), BF))
    grad_in, keep, send = run(
        last_body, (shape((own, d)),) + attn, part_sum, dk, dv, *dkv2, am0, ao0, sel, low, marks, vec01, vec02, vec1, vec2,
        name="last", scratch=(buf(tok, 2 * hw), buf(tok, 2 * hw)), after=(att1[0],),
    )
    att1 = send_on(att1, 1)
    key0 = halves(keep, send)
    att0 = join([query0, key0], after=(grad_in, ))
    ffn0 = add(ffn0, after=(att0[0], ))
    att0 = send_on(att0, 0)
    ffn0 = send_on(ffn0, 1)
    att0 = send_on(add(att0, after=(ffn0[0], att1[1], ffn1[1], )), 1)
    ffn1, att1, ffn0, att0 = [rest(x) for x in (ffn1, att1, ffn0, att0)]
    (grad_inputs,) = run(
        place_body, (shape((1, t, d)),), grad_in, flip(grad_in, "mp", 1), name="grad_inputs", scratch=(dma(2),), out_specs=(HB,)
    )
    res_out = to_role(res_out)
    outputs, bound_rows = run(
        put_body, (shape((1, t, d)), shape((1, spans, 2, d))), res_out, flip(res_out, "mp", 1),
        name="put", scratch=(pltpu.VMEM((spans, 2, d), F32), dma(3)), out_specs=(HB, HB),
    )

    def finish(layers, places, width, extra=(), name=None):
        outs = (shape((LAYERS, per, width)),) * len(places) + tuple(extra)
        return pl.pallas_call(
            finish_body(places, width, [len(x) for x in layers]), out_shape=outs,
            compiler_params=pltpu.CompilerParams(vmem_limit_bytes=LIMIT), name=name,
        )(*layers[0], *layers[1])

    g_outer, g_inner = finish((ffn0, ffn1), [(0, 0), (f, f)], f, name="finish_feed")
    vec_shape = shape((LAYERS, 2, per))
    at = 2 * hw
    g_output, g_query, g_key, g_value, g_gain, g_bias, g_mask = finish(
        (att0, att1), [(0, 0), (hw, hw), (at, 2 * hw), (at + hw, 3 * hw)], hw,
        (vec_shape, vec_shape, shape((1, per))), name="finish_attention",
    )
    return outputs, bound_rows, grad_inputs, g_mask, g_query, g_key, g_value, g_output, g_inner, g_outer, g_gain.transpose(0, 2, 1), g_bias.transpose(0, 2, 1)


def solution(mesh):
    row = P("dp", "seq", None)
    wide = P(None, None, "mp")
    out_w = P(None, ("dp", "seq"), "mp")
    out_v = P(None, ("dp", "seq"), None)
    return jax.shard_map(
        on_device,
        mesh=mesh,
        in_specs=(row, row, P(), wide, wide, wide, wide, wide, wide, P(), P(), row, P("dp", "seq", None, None)),
        out_specs=(row, P("dp", "seq", None, None), row, P(None, ("dp", "seq"))) + (out_w,) * 6 + (out_v,) * 2,
        check_vma=False,
    )
```

```python
import jax
import jax.numpy as jnp
from jax import lax
from jax.experimental import pallas as pl
from jax.experimental.pallas import tpu as pltpu
from jax.sharding import PartitionSpec as P

HD = 64
LAYERS = 2
EPS = 1e-12
SCALE = HD**-0.5
BF = jnp.bfloat16
F32 = jnp.float32
I32 = jnp.int32
LANES = 128
LIMIT = 3 * 2**20
BIG = 6 * 2**20
FORWARD = 15 * 2**20
RATE = 0.3e9
LONG = 8
COST = 12
GROUP = 6
VM = pl.BlockSpec(memory_space=pltpu.VMEM)
SM = pl.BlockSpec(memory_space=pltpu.SMEM)
HB = pl.BlockSpec(memory_space=pltpu.HBM)
ANY = pl.BlockSpec(memory_space=pl.ANY)


def shape(dims, kind=F32):
    return jax.ShapeDtypeStruct(tuple(dims), kind)


def run(body, outs, *args, name=None, smem=0, hbm=0, free=0, scratch=(), out_specs=None, limit=LIMIT, us=1.0, after=()):
    hbm_end = len(args) - free
    specs = [SM] * smem + [VM] * (hbm_end - smem - hbm) + [HB] * hbm + [ANY] * free + [pl.BlockSpec(memory_space=pl.ANY)] * len(after)
    count = len(args)
    held = tuple(pltpu.with_memory_space_constraint(a, pltpu.HBM) for a in args[hbm_end - hbm : hbm_end])
    args = args[: hbm_end - hbm] + held + args[hbm_end:]
    def whole(*refs):
        body(*refs[:count], *refs[count + len(after) :])

    return pl.pallas_call(
        whole,
        out_shape=tuple(outs),
        in_specs=specs,
        out_specs=(VM,) * len(outs) if out_specs is None else tuple(out_specs),
        scratch_shapes=scratch,
        compiler_params=pltpu.CompilerParams(vmem_limit_bytes=limit),
        cost_estimate=pl.CostEstimate(flops=int(us * RATE), bytes_accessed=1, transcendentals=0),
        name=name,
    )(*args, *after)


def dot(a, b, ca, cb):
    return lax.dot_general(a, b, (((ca,), (cb,)), ((), ())), preferred_element_type=F32)


def flip(x, axis, mask):
    count = lax.axis_size(axis)
    return lax.ppermute(x, axis, [(i, i ^ mask) for i in range(count)])


KEY, VALUE, QUERY, OUT = range(4)


def sides(own, other, n):
    return own.at[n], other.at[n]


def own_place(own):
    return lax.axis_index("seq") * (2 * own) + lax.axis_index("mp") * own


def load(layer, weights, packed, sems, first=0):
    copies = [pltpu.make_async_copy(w.at[layer], packed.at[i], sems.at[first + i]) for i, w in enumerate(weights)]
    for c in copies:
        c.start()
    return copies


def add_beside_body(keep, got, first, first_send, rest, send):
    n, w = rest.shape[0], first.shape[1]
    rest[:, :w] = first[...]
    send[:, :w] = first_send[...]
    rest[:, w:] = keep[0:n] + got[0:n].astype(F32)
    send[:, w:] = (keep[n:] + got[n:].astype(F32)).astype(BF)


def start_body(spans, mask_vector, inputs, grads, bounds, wk, wv, wq, wo, packet, attention, hid, mv, gv, bv, sems, wsems):
    own, d = hid.shape
    n = spans.shape[1]
    at = lax.axis_index("mp") * own
    copies = [
        pltpu.make_async_copy(inputs.at[0, pl.ds(at, own)], hid, sems.at[0]),
        pltpu.make_async_copy(mask_vector, mv.at[0], sems.at[1]),
        pltpu.make_async_copy(grads.at[0, pl.ds(at, own)], gv, sems.at[2]),
        pltpu.make_async_copy(bounds.at[0], bv, sems.at[3]),
    ]
    for c in copies:
        c.start()
    weights = load(0, (wk, wv, wq, wo), attention, wsems)
    pos = lax.broadcasted_iota(I32, (own, 1), 0) + own_place(own)
    lane = lax.broadcasted_iota(I32, (8, d), 1) % (2 * n)
    mask = pos < 0
    edges = jnp.zeros((8, d), I32)
    for i in range(n):
        a, e = spans[0, i, 0], spans[0, i, 0] + spans[0, i, 1]
        mask = mask | ((pos >= a) & (pos < e))
        edges = jnp.where(lane == 2 * i, a - 1, jnp.where(lane == 2 * i + 1, e, edges))
    upper = lax.broadcasted_iota(I32, (8, d), 0) < 4
    edges = jnp.where(upper, edges // 16, edges % 16).astype(F32)
    copies[0].wait()
    copies[1].wait()
    x = jnp.where(mask, mv[...], hid[...])
    packet[0:own] = x.astype(BF)
    copies[2].wait()
    copies[3].wait()
    packet[own : 2 * own] = gv[...].astype(BF)
    packet[2 * own :] = jnp.concatenate([bv[i] for i in range(n)] + [edges], axis=0).astype(BF)
    for c in weights:
        c.wait()


def load_body(wk, wv, wq, wo, wi, wu, attention, wi0, wu0, wi1, wu1, sems):
    copies = load(1, (wk, wv, wq, wo), attention, sems)
    for i, (w, layer, b) in enumerate(((wi, 0, wi0), (wu, 0, wu0), (wi, 1, wi1), (wu, 1, wu1))):
        copies.append(pltpu.make_async_copy(w.at[layer], b, sems.at[4 + i]))
        copies[-1].start()
    for c in copies:
        c.wait()


def kv_first_body(*refs):
    parts, (am, other, hid, low, k, v, ao, sems) = refs[:-8], refs[-8:]
    copies = [pltpu.make_async_copy(other.at[i], ao.at[i], sems.at[i]) for i in range(4)]
    for c in copies:
        c.start()
    r = hid.shape[0] // len(parts)
    for i, p in enumerate(parts):
        sl = slice(i * r, (i + 1) * r)
        hid[sl] = p[0:r].astype(F32)
        low[sl] = p[0:r]
    copies[KEY].wait()
    copies[VALUE].wait()
    kv_body(low, am, ao, k, v)
    copies[QUERY].wait()
    copies[OUT].wait()


def kv_body(low, am, ao, k, v):
    x = low[...]
    for out, n in ((k, KEY), (v, VALUE)):
        h = out.shape[1] // 2
        for i, w in enumerate(sides(am, ao, n)):
            out[:, i * h : (i + 1) * h] = dot(x, w[...], 1, 0).astype(BF)


def q_body(low, am, ao, q):
    h = q.shape[1] // 2
    x = low[...]
    for i, w in enumerate(sides(am, ao, QUERY)):
        q[:, i * h : (i + 1) * h] = (dot(x, w[...], 1, 0) * SCALE).astype(BF)


def halves_of_pair():
    lanes = lax.broadcasted_iota(I32, (1, LANES), 1) < HD
    rows = lax.broadcasted_iota(I32, (LANES, 1), 0) < HD
    return lanes, rows


def rows_of(own, oth, g):
    pairs = own.shape[1] // LANES
    g2 = (g + pairs // 2) % pairs
    return jnp.concatenate([own[:, g * LANES : (g + 1) * LANES], oth[:, g2 * LANES : (g2 + 1) * LANES]], axis=0)


def normalize(a):
    mu = jnp.mean(a, axis=-1, keepdims=True)
    sh = a - mu
    rstd = lax.rsqrt(jnp.mean(sh * sh, axis=-1, keepdims=True) + EPS)
    return sh * rstd, rstd


def attend(q, k, v, ko, vo, probs, mixed):
    width = q.shape[1]
    pairs = width // LANES
    lo, top = halves_of_pair()
    for g0 in range(0, pairs, GROUP):
        scores = []
        for g in range(g0, g0 + GROUP):
            qq = q[:, g * LANES : (g + 1) * LANES]
            kk = rows_of(k, ko, g)
            scores += [dot(kk, jnp.where(m, qq, 0), 1, 1) for m in (lo, ~lo)]
        exps = [jnp.exp(s - jnp.max(s, axis=0, keepdims=True)) for s in scores]
        low = [(e * (1.0 / jnp.sum(e, axis=0, keepdims=True))).astype(BF) for e in exps]
        for j in range(2 * GROUP):
            probs[2 * g0 + j] = low[j]
        for g in range(g0, g0 + GROUP):
            j = 2 * (g - g0)
            vv = rows_of(v, vo, g)
            r = jnp.where(top, dot(vv, low[j], 0, 0), dot(vv, low[j + 1], 0, 0))
            mixed[:, g * LANES : (g + 1) * LANES] = r.T.astype(BF)


def attend_out(hid, mixed, am, ao, gain, bias, n1, r1, ln):
    h = mixed.shape[1] // 2
    branch = None
    for i, w in enumerate(sides(am, ao, OUT)):
        y = dot(mixed[:, i * h : (i + 1) * h], w[...], 1, 1)
        branch = y if branch is None else branch + y
    n, r = normalize(hid[...] + branch)
    n1[...] = n
    r1[...] = r
    y = n * gain + bias
    ln[...] = y.astype(BF)
    return y


def ffn_half(x, i, wi, wu, act, dgelu):
    f = wi.shape[1]
    inner = dot(x, wi[...], 1, 0)
    cdf = 0.5 + 0.5 * lax.erf(inner * 0.7071067811865476)
    a = (inner * cdf).astype(BF)
    act[:, i * f : (i + 1) * f] = a
    dgelu[:, i * f : (i + 1) * f] = (cdf + inner * jnp.exp(-0.5 * inner * inner) * 0.3989422804014327).astype(BF)
    return dot(a, wu[...], 1, 1)


def norm_back(grad, n, rstd, gain):
    e = grad * gain
    back = (e - jnp.mean(e, axis=-1, keepdims=True) - n * jnp.mean(e * n, axis=-1, keepdims=True)) * rstd
    return back, jnp.sum(grad * n, axis=0, keepdims=True), jnp.sum(grad, axis=0, keepdims=True)


def weight_grad(sel, a, bs, keep, send, at=0):
    pick = dot(sel[...], a[...], 1, 1).astype(BF)
    for b in bs:
        h = b.shape[1] // 2
        keep[:, at : at + h] = dot(pick, b[:, :h], 1, 0)
        send[:, at : at + h] = dot(pick, b[:, h:], 1, 0).astype(BF)
        at += h


def attend_layer_body(layer):
    def body(q, k, v, ko, vo, hid, gains, biases, am, ao, probs, mixed, n1, r1, ln, y):
        attend(q, k, v, ko, vo, probs, mixed)
        y[...] = attend_out(hid, mixed, am, ao, gains[layer, 0:1], biases[layer, 0:1], n1, r1, ln)

    return body


def ffn_part_body(ln, wi, wu, act, dgelu, out):
    out[...] = ffn_half(ln[...], 0, wi, wu, act, dgelu).astype(out.dtype)


def ffn_end_body(y, part, got, gains, biases, am, ao, n2, r2, hid, low, k, v):
    n, r = normalize(y[...] + part[...] + got[...].astype(F32))
    n2[...] = n
    r2[...] = r
    x = n * gains[0, 1:2] + biases[0, 1:2]
    hid[...] = x
    low[...] = x.astype(BF)
    kv_body(low, am, ao, k, v)


def turn_body(y, part, got, gains, biases, grad, hid, mid, lmid, la, lb, vec):
    n, r = normalize(y[...] + part[...] + got[...].astype(F32))
    hid[...] = n * gains[1, 1:2] + biases[1, 1:2]
    middle_back(grad[...], n, r, gains[1, 1:2], mid, lmid, (la, lb), vec)


def rows_joined(pieces):
    return jnp.concatenate([p[...] for p in pieces], axis=0)


def store_rows(x, pieces):
    n = pieces[0].shape[0]
    for i, p in enumerate(pieces):
        p[...] = x[i * n : (i + 1) * n].astype(p.dtype)


def middle_back(grad, n, r, gain, mid, lmid, pieces, vec):
    back, gg, gb = norm_back(grad, n, r, gain)
    mid[...] = back
    lmid[...] = back.astype(BF)
    store_rows(back, pieces)
    vec[0:1] = gg
    vec[1:2] = gb


def ffn_back_own_body(lmid, dgelu, wi, wu, inner, out):
    g = (dot(lmid[...], wu[...], 1, 0) * dgelu[...].astype(F32)).astype(BF)
    inner[...] = g
    out[...] = dot(g, wi[...], 1, 1)


def ffn_back_other_body(la, lb, dgelu, wi, wu, inner, oa, ob):
    g = (dot(rows_joined((la, lb)), wu[...], 1, 0) * dgelu[...].astype(F32)).astype(BF)
    inner[...] = g
    store_rows(dot(g, wi[...], 1, 1), (oa, ob))


def weight_feed_body(sel, lmid, la, lb, ln, lno, act, acto, inner, innero, rest, send):
    n, f = rest.shape[0], act.shape[1]
    for i, (a, ao, b, bo) in enumerate(((lmid[...], rows_joined((la, lb)), act, acto), (ln[...], lno[...], inner, innero))):
        pick = dot(sel[...], a, 1, 1).astype(BF)
        picko = dot(sel[...], ao, 1, 1).astype(BF)
        g = dot(pick, b[...], 1, 0) + dot(picko, bo[...], 1, 0)
        rest[:, i * f : (i + 1) * f] = g[0:n]
        send[:, i * f : (i + 1) * f] = g[n:].astype(BF)


def ffn_back_end_body(layer):
    def body(mid, part, ga, gb, gains, n1, r1, am, ao, res, lres, mix, vec):
        total = mid[...] + part[...] + rows_joined((ga, gb)).astype(F32)
        back, gain_sum, bias_sum = norm_back(total, n1[...], r1[...], gains[layer, 0:1])
        res[...] = back
        low = back.astype(BF)
        lres[...] = low
        vec[0:1] = gain_sum
        vec[1:2] = bias_sum
        h = mix.shape[1] // 2
        for i, w in enumerate(sides(am, ao, OUT)):
            mix[:, i * h : (i + 1) * h] = dot(low, w[...], 1, 0).astype(BF)

    return body


def grad_one_body(sel, a, b, keep, send):
    weight_grad(sel, a, (b,), keep, send)


def grad_two_body(sel, a, b, c, d, keep, send):
    weight_grad(sel, a, (b,), keep, send)
    weight_grad(sel, c, (d,), keep, send, b.shape[1] // 2)


def attend_back_body(mix, mixed, probs, q, v, vo, dscores, *theirs):
    t, width = q.shape
    pairs = width // LANES
    lo, top = halves_of_pair()
    for g in range(pairs):
        sl = slice(g * LANES, (g + 1) * LANES)
        gg = mix[:, sl]
        vv = rows_of(v, vo, g)
        delta = (gg.astype(F32) * mixed[:, sl].astype(F32)).T
        ds = []
        for j, m in enumerate((lo, ~lo)):
            dl = jnp.sum(delta[j * HD : (j + 1) * HD], axis=0, keepdims=True)
            dp = dot(vv, jnp.where(m, gg, 0), 1, 1)
            ds.append((probs[2 * g + j].astype(F32) * (dp - dl)).astype(BF))
            dscores[2 * g + j] = ds[j]
        qq = q[:, sl]
        at = (g + pairs // 2) % pairs * LANES
        count = len(theirs) // 2
        dk, dv = theirs[at * count // width], theirs[count + at * count // width]
        at = at % (width // count)
        to = slice(at, at + LANES)
        dk[:, to] = jnp.where(lo, dot(ds[0][t:], qq, 1, 0), dot(ds[1][t:], qq, 1, 0)).astype(BF)
        dv[:, to] = jnp.where(lo, dot(probs[2 * g, t:], gg, 1, 0), dot(probs[2 * g + 1, t:], gg, 1, 0)).astype(BF)


def attend_back_own(mix, probs, dscores, q, k, ko, res, am, ao, dk, dv, gq, rest):
    t, width = q.shape
    pairs = width // LANES
    lo, top = halves_of_pair()
    for g in range(pairs):
        sl = slice(g * LANES, (g + 1) * LANES)
        gg, qq = mix[:, sl], q[:, sl]
        kk = rows_of(k, ko, g)
        dq = jnp.where(top, dot(kk, dscores[2 * g], 0, 0), dot(kk, dscores[2 * g + 1], 0, 0))
        gq[:, sl] = (dq * SCALE).T.astype(BF)
        dk[:, sl] = jnp.where(lo, dot(dscores[2 * g, :t], qq, 1, 0), dot(dscores[2 * g + 1, :t], qq, 1, 0))
        dv[:, sl] = jnp.where(lo, dot(probs[2 * g, :t], gg, 1, 0), dot(probs[2 * g + 1, :t], gg, 1, 0))
    h = width // 2
    total = res[...]
    for i, w in enumerate(sides(am, ao, QUERY)):
        total = total + dot(gq[:, i * h : (i + 1) * h], w[...], 1, 1)
    rest[...] = total


def hidden_back(rest, dk, dv, ka, kb, va, vb, am, ao, gk, gv):
    total = rest[...]
    for own, theirs, out, n in ((dk, (ka, kb), gk, KEY), (dv, (va, vb), gv, VALUE)):
        h = out.shape[1] // 2
        for i, w in enumerate(sides(am, ao, n)):
            sl = slice(i * h, (i + 1) * h)
            g = (own[:, sl] + theirs[i][...].astype(F32)).astype(BF)
            out[:, sl] = g
            total = total + dot(g, w[...], 1, 1)
    return total


def next_layer_body(rest, dk, dv, ka, kb, va, vb, am, ao, n2, r2, gains, gk, gv, mid, lmid, la, lb, vec):
    grad = hidden_back(rest, dk, dv, ka, kb, va, vb, am, ao, gk, gv)
    middle_back(grad, n2[...], r2[...], gains[0, 1:2], mid, lmid, (la, lb), vec)


def grad_attention_body(sel, lres, mixed, low, gq, gk, gv, keep, send, keep2, send2):
    weight_grad(sel, lres, (mixed,), keep, send)
    weight_grad(sel, low, (gq,), keep, send, mixed.shape[1] // 2)
    weight_grad(sel, low, (gk, gv), keep2, send2)


def split_dot(onehot, x, ca, cb):
    total = None
    for _ in range(3):
        part = x.astype(BF)
        x = x - part.astype(F32)
        y = dot(onehot, part, ca, cb)
        total = y if total is None else total + y
    return total


def last_body(rest, dk, dv, dk2, dv2, am, ao, sel, low, marks, v1, v2, v3, v4, grad_in, keep, send, gk, gv):
    w = gk.shape[1]
    own, h = grad_in.shape[0], w // 2
    grad = hidden_back(rest, dk, dv, dk2[:, :h], dk2[:, h:], dv2[:, :h], dv2[:, h:], am, ao, gk, gv)
    weight_grad(sel, low, (gk, gv), keep, send)
    grad_in[...] = jnp.where(marks[0:own, 0:1] > 0.5, 0.0, grad[0:own])
    mask = jnp.sum(grad * marks[:, 0:1], axis=0, keepdims=True)
    rows = jnp.concatenate([v1[...], v2[...], v3[...], v4[...], jnp.broadcast_to(mask, (8,) + mask.shape[1:])], axis=0)
    rows = jnp.concatenate([rows, jnp.zeros((LANES - rows.shape[0], rows.shape[1]), F32)], axis=0)
    small = split_dot(sel[...], rows, 1, 1)
    keep[:, w:] = small
    send[:, w:] = small.astype(BF)


def join_body(parts):
    def body(*refs):
        keeps, gots, rest, sends = refs[:parts], refs[parts : 2 * parts], refs[2 * parts], refs[2 * parts + 1 :]
        n, at = rest.shape[0], 0
        for keep, got in zip(keeps, gots):
            to = slice(at, at + keep.shape[1])
            rest[:, to] = keep[0:n] + got[0:n].astype(F32)
            for i, x in enumerate(sends):
                sl = slice((i + 1) * n, (i + 2) * n)
                x[:, to] = (keep[sl] + got[sl].astype(F32)).astype(BF)
            at += keep.shape[1]

    return body


def add_body(keep, got, rest, send):
    n = rest.shape[0]
    rest[...] = keep[0:n] + got[0:n].astype(F32)
    send[...] = (keep[n:] + got[n:].astype(F32)).astype(BF)


def top_body(*refs):
    n = len(refs) - 2
    parts, (grad, marks) = refs[:n], refs[n:]
    h = grad.shape[0] // n
    lane = lax.broadcasted_iota(I32, (1, LANES), 1)
    edges = jnp.full((1, LANES), -8.0, F32)
    bounds = []
    for j, p in enumerate(parts):
        tail = p[2 * h :].astype(F32)
        b = tail.shape[0] - 8
        edges = jnp.where((lane >= j * b) & (lane < (j + 1) * b), edges_of(tail), edges)
        bounds.append(tail[0:b])
    bounds = jnp.concatenate(bounds, axis=0)
    bounds = jnp.concatenate([bounds, jnp.zeros((LANES - bounds.shape[0], bounds.shape[1]), F32)], axis=0).astype(BF)
    row = lax.broadcasted_iota(I32, (h, 1), 0)
    even = (lane % 2) == 0
    for j, p in enumerate(parts):
        pos = (row + block_place(j, h)).astype(F32)
        onehot = jnp.where(pos == edges, 1.0, 0.0).astype(BF)
        grad[j * h : (j + 1) * h] = p[h : 2 * h].astype(F32) + dot(onehot, bounds, 1, 0)
        after = jnp.where((even & (pos > edges)) & (edges > -4.0), 1.0, 0.0) - jnp.where((~even & (pos >= edges)) & (edges > -4.0), 1.0, 0.0)
        marks[j * h : (j + 1) * h] = jnp.broadcast_to(jnp.sum(after, axis=1, keepdims=True), (h, LANES))


def block_place(j, own):
    return (lax.axis_index("seq") ^ j) * (2 * own) + lax.axis_index("mp") * own


def edges_of(payload):
    e = payload[-8:, 0:LANES].astype(F32)
    return e[0:1] * 16.0 + e[4:5]


def result_body(hid, payload, out):
    own = hid.shape[0] // lax.axis_size("seq")
    n = out.shape[0] - own
    out[0:own] = hid[0:own]
    row = jnp.broadcast_to(edges_of(payload), (8, LANES)).T[0:n, 0:1]
    lane = lax.broadcasted_iota(I32, (1, own), 1)
    total = None
    for j in range(hid.shape[0] // own):
        pos = (lane + block_place(j, own)).astype(F32)
        onehot = jnp.where(row == pos, 1.0, 0.0).astype(BF)
        y = split_dot(onehot, hid[j * own : (j + 1) * own], 1, 0)
        total = y if total is None else total + y
    out[own:] = total


def put_body(mine, other, out, bound, rows, sems):
    n = bound.shape[1] * 2
    own = mine.shape[0] - n
    m = lax.axis_index("mp")
    a = pltpu.make_async_copy(mine.at[0:own], out.at[0, pl.ds(m * own, own)], sems.at[0])
    b = pltpu.make_async_copy(other.at[0:own], out.at[0, pl.ds((1 - m) * own, own)], sems.at[1])
    a.start()
    b.start()
    total = mine[own:] + other[own:]
    for i in range(n // 2):
        rows[i] = total[2 * i : 2 * i + 2]
    c = pltpu.make_async_copy(rows, bound.at[0], sems.at[2])
    c.start()
    a.wait()
    b.wait()
    c.wait()


def place_body(mine, other, out, sems):
    own = mine.shape[0]
    m = lax.axis_index("mp")
    a = pltpu.make_async_copy(mine, out.at[0, pl.ds(m * own, own)], sems.at[0])
    b = pltpu.make_async_copy(other, out.at[0, pl.ds((1 - m) * own, own)], sems.at[1])
    a.start()
    b.start()
    a.wait()
    b.wait()


def finish_body(places, width, terms):
    def body(*refs):
        layers, outs = (refs[: terms[0]], refs[terms[0] : sum(terms)]), refs[sum(terms) :]

        def total(i, sl):
            x = layers[i][0][:, sl]
            for r in layers[i][1:]:
                x = x + r[:, sl].astype(F32)
            return x

        for i in range(LAYERS):
            for j, at in enumerate(places):
                outs[j][i] = total(i, slice(at[i], at[i] + width))
        if len(outs) > len(places):
            gain, bias, mask = outs[len(places) :]
            small = total(0, slice(4 * width, 4 * width + LANES)).T
            for i in range(LAYERS):
                for j in range(2):
                    at = 4 * i + 2 * j
                    gain[i, j : j + 1] = small[at : at + 1]
                    bias[i, j : j + 1] = small[at + 1 : at + 2]
            mask[...] = small[8:9]

    return body


def order_of(masks):
    if not masks:
        return [0]
    rest = order_of(masks[1:])
    return rest + [r ^ masks[0] for r in rest]


def tie(x, *others):
    return lax.optimization_barrier((x,) + others)[0]


def on_device(inputs, span_info, mask_vector, w_query, w_key, w_value, w_output, w_inner, w_outer, norm_gain, norm_bias, grad_output, grad_bounds):
    t, d = inputs.shape[1:]
    ns, nd = lax.axis_size("seq"), lax.axis_size("dp")
    s, z = lax.axis_index("seq"), lax.axis_index("dp")
    f = w_inner.shape[2]
    hw = w_query.shape[2]
    heads = 2 * hw // HD
    own = t // 2
    tok = own * ns
    axes = ("dp", "seq")
    masks = []
    bit = ns
    while bit < ns * nd:
        masks.append(bit)
        bit *= 2
    here = z * ns + s
    dma = lambda n: pltpu.SemaphoreType.DMA((n,))
    buf = lambda *dims: pltpu.VMEM(dims, BF)

    def to_role(x):
        return x

    def gather(x):
        return [x] + [flip(x, axes, j) for j in range(1, ns)]

    spans = span_info.shape[1]
    def other(*xs):
        return [flip(x, "mp", 1) for x in xs]

    weights = (w_key, w_value, w_query, w_output)
    attention = shape((4, d, hw), BF)
    packet, am0 = run(
        start_body, (shape((2 * own + 2 * spans + 8, d), BF), attention),
        span_info, mask_vector, inputs, grad_output, grad_bounds, *weights, name="start", smem=1, hbm=8,
        scratch=(pltpu.VMEM((own, d), F32), pltpu.VMEM((1, d), F32), pltpu.VMEM((own, d), F32), pltpu.VMEM((spans, 2, d), F32),
                 dma(4), dma(4)),
    )
    held0 = other(am0)[0]
    packets = gather(packet)
    feed_weight = shape((d, f), BF)
    am1, wi0, wu0, wi1, wu1 = run(
        load_body, (attention,) + (feed_weight,) * 4, *weights, w_inner, w_outer, name="load", hbm=6, scratch=(dma(8),), after=(packet,)
    )

    per = d // (ns * nd)
    base = jnp.concatenate([(here ^ r) * per + jnp.arange(per, dtype=I32) for r in order_of(masks)])
    sel = (base[:, None] == jnp.arange(d, dtype=I32)[None, :]).astype(BF)
    picks = sel.shape[0]
    gains, biases = norm_gain.transpose(0, 2, 1), norm_bias.transpose(0, 2, 1)

    full = shape((tok, d))
    full_low = shape((tok, d), BF)
    column = shape((tok, 1))
    wide = shape((tok, 2 * f), BF)
    kv_shape = shape((tok, 4 * hw), BF)
    prob_shape = shape((heads, 2 * tok, tok), BF)
    piece = (shape((picks, f)), shape((picks, f), BF))
    two = shape((2, d))

    hid, low, k, v, ao0 = run(
        kv_first_body, (full, full_low, full_low, full_low, attention), *packets, am0, held0,
        name="keys_first", hbm=1, scratch=(dma(4),), after=(sel, am1),
    )
    ko, vo = other(k, v)
    (q,) = run(q_body, (full_low,), low, am0, ao0, name="queries")
    ao1 = other(tie(am1, ko, vo))[0]
    narrow = shape((tok, f), BF)

    def attend_layer(layer, q, k, v, ko, vo, hid, am, ao):
        return run(
            attend_layer_body(layer), (prob_shape, full_low, full, column, full_low, full),
            q, k, v, ko, vo, hid, gains, biases, am, ao, name="attend", limit=BIG,
        )

    def ffn(ln, wi, wu):
        lno = other(ln)[0]
        act, dgelu, part = run(ffn_part_body, (narrow, narrow, full), ln, wi, wu, name="ffn_own")
        acto, dgeluo, parto = run(ffn_part_body, (narrow, narrow, full_low), lno, wi, wu, name="ffn_other", after=(part,))
        return lno, act, dgelu, acto, dgeluo, part, other(parto)[0]

    probs, mixed, n1, r1, ln, y = attend_layer(0, q, k, v, ko, vo, hid, am0, ao0)
    lno, act, dgelu, acto, dgeluo, part, got = ffn(ln, wi0, wu0)
    n2, r2, hid, low1, k1, v1 = run(
        ffn_end_body, (full, column, full, full_low, full_low, full_low), y, part, got, gains, biases, am1, ao1, name="ffn_end"
    )
    k1o, v1o = other(k1, v1)
    grad, marks = run(top_body, (full, shape((tok, LANES))), *packets, name="top", after=(k1,))
    (q1,) = run(q_body, (full_low,), low1, am1, ao1, name="queries", after=(grad,))
    probs1, mixed1, n11, r11, ln1, y = attend_layer(1, q1, k1, v1, k1o, v1o, hid, am1, ao1)
    ln1o, act1, dgelu1, act1o, dgelu1o, part, got = ffn(ln1, wi1, wu1)
    halved = (shape((tok // 2, d), BF),) * 2
    hid, mid, lmid, la, lb, vec2 = run(turn_body, (full, full, full_low) + halved + (two,), y, part, got, gains, biases, grad, name="turn")

    def join(pairs, blocks=2, after=()):
        width = sum(k.shape[1] for k, _ in pairs)
        n = picks // blocks
        return run(
            join_body(len(pairs)), (shape((n, width)),) + (shape((n, width), BF),) * (blocks - 1),
            *[k for k, _ in pairs], *[g for _, g in pairs], name="join", after=after,
        )

    def spread(pairs, after=()):
        if nd > 4:
            pair = send_on(join(pairs, after=after), 0)
            for i in range(1, len(masks)):
                pair = send_on(add(pair), i)
            return pair
        keep, *sends = join(pairs, nd, after=after)
        return [keep] + [flip(x, axes, o) for x, o in zip(sends, order_of(masks)[1:])]

    def send_on(pair, step):
        return pair[0], flip(pair[1], axes, masks[step])

    def add(pair, after=(), us=1.0):
        keep, got = pair
        n, w = keep.shape[0] // 2, keep.shape[1]
        if n % 16:
            total = keep + got.astype(F32)
            return total[:n], total[n:].astype(BF)
        return run(add_body, (shape((n, w)), shape((n, w), BF)), keep, got, name="add", after=after, us=us)

    def rest(pair):
        for i in range(2, len(masks)):
            pair = send_on(add(pair), i)
        return pair

    def halves(keep, send):
        return keep, flip(send, "mp", 1)

    group = (shape((picks // 2, 2 * f)), shape((picks // 2, 2 * f), BF))

    def ffn_back(layer, mid, lmid, lmids, dgelu, dgeluo, wi, wu, n1, r1, am, ao, after=(), between=None):
        lmids = other(*lmids)
        inner, part = run(ffn_back_own_body, (narrow, full), lmid, dgelu, wi, wu, name="ffn_back_own", after=after)
        innero, *parts = run(
            ffn_back_other_body, (narrow,) + halved, *lmids, dgeluo, wi, wu, name="ffn_back_other", after=(part,)
        )
        gots = other(*parts)
        ends = run(
            ffn_back_end_body(layer), (full, full_low, full_low, two), mid, part, *gots, gains, n1, r1, am, ao,
            name="ffn_back_end", after=between(lmids, inner, innero),
        )
        return (lmids, inner, innero) + tuple(ends)

    def grad_feed(lmid, lmids, ln, lno, act, acto, inner, innero, after=()):
        return run(weight_feed_body, group, sel, lmid, *lmids, ln, lno, act, acto, inner, innero, name="grad_feed", after=after)

    def attend_own(mix, probs, dscores, q, k, ko, res, am, ao, after=()):
        return run(
            attend_back_own, (full, full, full_low, full), mix, probs, dscores, q, k, ko, res, am, ao,
            name="attend_back_own", after=after,
        )

    def attend_back(mix, mixed, probs, q, v, vo, after=()):
        return run(
            attend_back_body, (prob_shape, shape((tok, 4 * hw), BF)), mix, mixed, probs, q, v, vo, name="attend_back", us=2.3, after=after
        )

    def grad_pair(a, b, after=(), name=None, us=0.9):
        w = b.shape[1] // 2
        return run(grad_one_body, (shape((picks, w)), shape((picks, w), BF)), sel, a, b, name=name, us=us, after=after)

    sums = {}

    def between(lmids, inner, innero):
        sums["ffn"] = grad_feed(lmid, lmids, ln1, ln1o, act1, act1o, inner, innero)
        return (sums["ffn"][0],)

    _, _, _, res, lres1, mix, vec1 = ffn_back(
        1, mid, lmid, (la, lb), dgelu1, dgelu1o, wi1, wu1, n11, r11, am1, ao1, between=between
    )
    ffn1 = send_on(sums["ffn"], 0)
    theirs = (shape((tok, hw), BF),) * 4
    dscores, *dkv2 = run(attend_back_body, (prob_shape,) + theirs, mix, mixed1, probs1, q1, v1, v1o, name="attend_back")
    dkv2 = other(*dkv2)
    dk, dv, gq, part_sum = attend_own(mix, probs1, dscores, q1, k1, k1o, res, am1, ao1)
    gk, gv, mid, lmid, la, lb, vec02 = run(
        next_layer_body, (full_low, full_low, full, full_low) + halved + (two,), part_sum, dk, dv, *dkv2, am1, ao1, n2, r2, gains, name="next_layer"
    )
    attn = (shape((picks, 2 * hw)), shape((picks, 2 * hw), BF))
    keep, send, keep2, send2 = run(
        grad_attention_body, attn * 2, sel, lres1, mixed1, low1, gq, gk, gv, name="grad_attention", after=(mid,)
    )
    att1 = halves(keep, send), halves(keep2, send2)
    def between(lmids, inner, innero):
        sums["ffn"] = add(ffn1, after=(innero,))
        sums["attention"] = join(att1, after=(sums["ffn"][0],))
        return (sums["attention"][0],)

    lmids, inner, innero, res, lres0, mix, vec01 = ffn_back(
        0, mid, lmid, (la, lb), dgelu, dgeluo, wi0, wu0, n1, r1, am0, ao0, after=(keep,), between=between
    )
    att1 = send_on(sums["attention"], 0)
    dscores, *dkv2 = run(attend_back_body, (prob_shape, full_low, full_low), mix, mixed, probs, q, v, vo, name="attend_back")
    dkv2 = other(*dkv2)
    ffn0 = grad_feed(lmid, lmids, ln, lno, act, acto, inner, innero, after=(dscores,))
    (keep, got), (first, first_send) = att1, sums["ffn"]
    n, w = first.shape[0], first.shape[1] + keep.shape[1]
    layer1 = run(
        add_beside_body, (shape((n, w)), shape((n, w), BF)), keep, got, first, first_send, name="add_beside", us=LONG, after=(ffn0[0],)
    )
    (res_out,) = run(result_body, (shape((own + 2 * spans, d)),), hid, packets[0], name="result", after=(layer1[0],))
    ffn0 = send_on(ffn0, 0)
    layer1 = send_on(layer1, 1)
    dk, dv, gq, part_sum = attend_own(mix, probs, dscores, q, k, ko, res, am0, ao0, after=(res_out,))
    query0 = halves(*run(
        grad_two_body, (shape((picks, 2 * hw)), shape((picks, 2 * hw), BF)), sel, lres0, mixed, low, gq, name="grad_query"
    ))
    attn = (shape((picks, 2 * hw + LANES)), shape((picks, 2 * hw + LANES), BF))
    grad_in, keep, send = run(
        last_body, (shape((own, d)),) + attn, part_sum, dk, dv, *dkv2, am0, ao0, sel, low, marks, vec01, vec02, vec1, vec2,
        name="last", scratch=(buf(tok, 2 * hw), buf(tok, 2 * hw)), after=(query0[0],),
    )
    key0 = halves(keep, send)
    att0 = join([query0, key0], after=(grad_in,))
    ffn0 = add(ffn0, after=(att0[0], layer1[1]), us=COST)
    att0 = send_on(att0, 0)
    ffn0 = send_on(ffn0, 1)
    att0 = send_on(add(att0, after=(ffn0[0],)), 1)
    layer1, ffn0, att0 = [rest(x) for x in (layer1, ffn0, att0)]
    (grad_inputs,) = run(
        place_body, (shape((1, t, d)),), grad_in, flip(grad_in, "mp", 1), name="grad_inputs", scratch=(dma(2),), out_specs=(HB,)
    )
    res_out = to_role(res_out)
    outputs, bound_rows = run(
        put_body, (shape((1, t, d)), shape((1, spans, 2, d))), res_out, flip(res_out, "mp", 1),
        name="put", scratch=(pltpu.VMEM((spans, 2, d), F32), dma(3)), out_specs=(HB, HB),
    )

    def finish(layers, places, width, extra=(), name=None):
        outs = (shape((LAYERS, per, width)),) * len(places) + tuple(extra)
        return pl.pallas_call(
            finish_body(places, width, [len(x) for x in layers]), out_shape=outs,
            compiler_params=pltpu.CompilerParams(vmem_limit_bytes=LIMIT), name=name,
        )(*layers[0], *layers[1])

    g_outer, g_inner = finish((ffn0, layer1), [(0, 0), (f, f)], f, name="finish_feed")
    vec_shape = shape((LAYERS, 2, per))
    at = 2 * hw
    g_output, g_query, g_key, g_value, g_gain, g_bias, g_mask = finish(
        (att0, layer1), [(0, 2 * f), (hw, 2 * f + hw), (at, 2 * f + at), (at + hw, 2 * f + at + hw)], hw,
        (vec_shape, vec_shape, shape((1, per))), name="finish_attention",
    )
    return outputs, bound_rows, grad_inputs, g_mask, g_query, g_key, g_value, g_output, g_inner, g_outer, g_gain.transpose(0, 2, 1), g_bias.transpose(0, 2, 1)


def solution(mesh):
    row = P("dp", "seq", None)
    wide = P(None, None, "mp")
    out_w = P(None, ("dp", "seq"), "mp")
    out_v = P(None, ("dp", "seq"), None)
    return jax.shard_map(
        on_device,
        mesh=mesh,
        in_specs=(row, row, P(), wide, wide, wide, wide, wide, wide, P(), P(), row, P("dp", "seq", None, None)),
        out_specs=(row, P("dp", "seq", None, None), row, P(None, ("dp", "seq"))) + (out_w,) * 6 + (out_v,) * 2,
        check_vma=False,
    )
```

```python
import jax
import jax.numpy as jnp
from jax import lax
from jax.experimental import pallas as pl
from jax.experimental.pallas import tpu as pltpu
from jax.sharding import PartitionSpec as P

HD = 64
LAYERS = 2
EPS = 1e-12
SCALE = HD**-0.5
BF = jnp.bfloat16
F32 = jnp.float32
I32 = jnp.int32
LANES = 128
LIMIT = 3 * 2**20
BIG = 6 * 2**20
FORWARD = 15 * 2**20
RATE = 0.3e9
LONG = 8
COST = 12
GROUP = 6
VM = pl.BlockSpec(memory_space=pltpu.VMEM)
SM = pl.BlockSpec(memory_space=pltpu.SMEM)
HB = pl.BlockSpec(memory_space=pltpu.HBM)
ANY = pl.BlockSpec(memory_space=pl.ANY)


def shape(dims, kind=F32):
    return jax.ShapeDtypeStruct(tuple(dims), kind)


def run(body, outs, *args, name=None, smem=0, hbm=0, free=0, scratch=(), out_specs=None, limit=LIMIT, us=1.0, after=()):
    hbm_end = len(args) - free
    specs = [SM] * smem + [VM] * (hbm_end - smem - hbm) + [HB] * hbm + [ANY] * free + [pl.BlockSpec(memory_space=pl.ANY)] * len(after)
    count = len(args)
    held = tuple(pltpu.with_memory_space_constraint(a, pltpu.HBM) for a in args[hbm_end - hbm : hbm_end])
    args = args[: hbm_end - hbm] + held + args[hbm_end:]
    def whole(*refs):
        body(*refs[:count], *refs[count + len(after) :])

    return pl.pallas_call(
        whole,
        out_shape=tuple(outs),
        in_specs=specs,
        out_specs=(VM,) * len(outs) if out_specs is None else tuple(out_specs),
        scratch_shapes=scratch,
        compiler_params=pltpu.CompilerParams(vmem_limit_bytes=limit),
        cost_estimate=pl.CostEstimate(flops=int(us * RATE), bytes_accessed=1, transcendentals=0),
        name=name,
    )(*args, *after)


def dot(a, b, ca, cb):
    return lax.dot_general(a, b, (((ca,), (cb,)), ((), ())), preferred_element_type=F32)


def flip(x, axis, mask):
    count = lax.axis_size(axis)
    return lax.ppermute(x, axis, [(i, i ^ mask) for i in range(count)])


KEY, VALUE, QUERY, OUT = range(4)


def sides(own, other, n):
    return own.at[n], other.at[n]


def own_place(own):
    return lax.axis_index("seq") * (2 * own) + lax.axis_index("mp") * own


def load(layer, weights, packed, sems, first=0):
    copies = [pltpu.make_async_copy(w.at[layer], packed.at[i], sems.at[first + i]) for i, w in enumerate(weights)]
    for c in copies:
        c.start()
    return copies


def add_beside_body(keep, got, first, first_send, rest, send):
    n, w = rest.shape[0], first.shape[1]
    rest[:, :w] = first[...]
    send[:, :w] = first_send[...]
    rest[:, w:] = keep[0:n] + got[0:n].astype(F32)
    send[:, w:] = (keep[n:] + got[n:].astype(F32)).astype(BF)


def start_body(spans, mask_vector, inputs, grads, bounds, wk, wv, wq, wo, packet, attention, hid, mv, gv, bv, sems, wsems):
    own, d = hid.shape
    n = spans.shape[1]
    at = lax.axis_index("mp") * own
    copies = [
        pltpu.make_async_copy(inputs.at[0, pl.ds(at, own)], hid, sems.at[0]),
        pltpu.make_async_copy(mask_vector, mv.at[0], sems.at[1]),
        pltpu.make_async_copy(grads.at[0, pl.ds(at, own)], gv, sems.at[2]),
        pltpu.make_async_copy(bounds.at[0], bv, sems.at[3]),
    ]
    for c in copies:
        c.start()
    weights = load(0, (wk, wv, wq, wo), attention, wsems)
    pos = lax.broadcasted_iota(I32, (own, 1), 0) + own_place(own)
    lane = lax.broadcasted_iota(I32, (8, d), 1) % (2 * n)
    mask = pos < 0
    edges = jnp.zeros((8, d), I32)
    for i in range(n):
        a, e = spans[0, i, 0], spans[0, i, 0] + spans[0, i, 1]
        mask = mask | ((pos >= a) & (pos < e))
        edges = jnp.where(lane == 2 * i, a - 1, jnp.where(lane == 2 * i + 1, e, edges))
    upper = lax.broadcasted_iota(I32, (8, d), 0) < 4
    edges = jnp.where(upper, edges // 16, edges % 16).astype(F32)
    copies[0].wait()
    copies[1].wait()
    x = jnp.where(mask, mv[...], hid[...])
    packet[0:own] = x.astype(BF)
    copies[2].wait()
    copies[3].wait()
    packet[own : 2 * own] = gv[...].astype(BF)
    packet[2 * own :] = jnp.concatenate([bv[i] for i in range(n)] + [edges], axis=0).astype(BF)
    for c in weights:
        c.wait()


def load_body(wk, wv, wq, wo, wi, wu, attention, wi0, wu0, wi1, wu1, sems):
    copies = load(1, (wk, wv, wq, wo), attention, sems)
    for i, (w, layer, b) in enumerate(((wi, 0, wi0), (wu, 0, wu0), (wi, 1, wi1), (wu, 1, wu1))):
        copies.append(pltpu.make_async_copy(w.at[layer], b, sems.at[4 + i]))
        copies[-1].start()
    for c in copies:
        c.wait()


def kv_first_body(*refs):
    parts, (am, other, hid, low, k, v, ao, sems) = refs[:-8], refs[-8:]
    copies = [pltpu.make_async_copy(other.at[i], ao.at[i], sems.at[i]) for i in range(4)]
    for c in copies:
        c.start()
    r = hid.shape[0] // len(parts)
    for i, p in enumerate(parts):
        sl = slice(i * r, (i + 1) * r)
        hid[sl] = p[0:r].astype(F32)
        low[sl] = p[0:r]
    copies[KEY].wait()
    copies[VALUE].wait()
    kv_body(low, am, ao, k, v)
    copies[QUERY].wait()
    copies[OUT].wait()


def kv_body(low, am, ao, k, v):
    x = low[...]
    for out, n in ((k, KEY), (v, VALUE)):
        h = out.shape[1] // 2
        for i, w in enumerate(sides(am, ao, n)):
            out[:, i * h : (i + 1) * h] = dot(x, w[...], 1, 0).astype(BF)


def q_body(low, am, ao, q):
    h = q.shape[1] // 2
    x = low[...]
    for i, w in enumerate(sides(am, ao, QUERY)):
        q[:, i * h : (i + 1) * h] = (dot(x, w[...], 1, 0) * SCALE).astype(BF)


def halves_of_pair():
    lanes = lax.broadcasted_iota(I32, (1, LANES), 1) < HD
    rows = lax.broadcasted_iota(I32, (LANES, 1), 0) < HD
    return lanes, rows


def rows_of(own, oth, g):
    pairs = own.shape[1] // LANES
    g2 = (g + pairs // 2) % pairs
    return jnp.concatenate([own[:, g * LANES : (g + 1) * LANES], oth[:, g2 * LANES : (g2 + 1) * LANES]], axis=0)


def normalize(a):
    mu = jnp.mean(a, axis=-1, keepdims=True)
    sh = a - mu
    rstd = lax.rsqrt(jnp.mean(sh * sh, axis=-1, keepdims=True) + EPS)
    return sh * rstd, rstd


def attend(q, k, v, ko, vo, probs, mixed):
    width = q.shape[1]
    pairs = width // LANES
    lo, top = halves_of_pair()
    for g0 in range(0, pairs, GROUP):
        scores = []
        for g in range(g0, g0 + GROUP):
            qq = q[:, g * LANES : (g + 1) * LANES]
            kk = rows_of(k, ko, g)
            scores += [dot(kk, jnp.where(m, qq, 0), 1, 1) for m in (lo, ~lo)]
        exps = [jnp.exp(s - jnp.max(s, axis=0, keepdims=True)) for s in scores]
        low = [(e * (1.0 / jnp.sum(e, axis=0, keepdims=True))).astype(BF) for e in exps]
        for j in range(2 * GROUP):
            probs[2 * g0 + j] = low[j]
        for g in range(g0, g0 + GROUP):
            j = 2 * (g - g0)
            vv = rows_of(v, vo, g)
            r = jnp.where(top, dot(vv, low[j], 0, 0), dot(vv, low[j + 1], 0, 0))
            mixed[:, g * LANES : (g + 1) * LANES] = r.T.astype(BF)


def attend_out(hid, mixed, am, ao, gain, bias, n1, r1, ln):
    h = mixed.shape[1] // 2
    branch = None
    for i, w in enumerate(sides(am, ao, OUT)):
        y = dot(mixed[:, i * h : (i + 1) * h], w[...], 1, 1)
        branch = y if branch is None else branch + y
    n, r = normalize(hid[...] + branch)
    n1[...] = n
    r1[...] = r
    y = n * gain + bias
    ln[...] = y.astype(BF)
    return y


def ffn_half(x, i, wi, wu, act, dgelu):
    f = wi.shape[1]
    inner = dot(x, wi[...], 1, 0)
    cdf = 0.5 + 0.5 * lax.erf(inner * 0.7071067811865476)
    a = (inner * cdf).astype(BF)
    act[:, i * f : (i + 1) * f] = a
    dgelu[:, i * f : (i + 1) * f] = (cdf + inner * jnp.exp(-0.5 * inner * inner) * 0.3989422804014327).astype(BF)
    return dot(a, wu[...], 1, 1)


def norm_back(grad, n, rstd, gain):
    e = grad * gain
    back = (e - jnp.mean(e, axis=-1, keepdims=True) - n * jnp.mean(e * n, axis=-1, keepdims=True)) * rstd
    return back, jnp.sum(grad * n, axis=0, keepdims=True), jnp.sum(grad, axis=0, keepdims=True)


def weight_grad(sel, a, bs, keep, send, at=0):
    pick = dot(sel[...], a[...], 1, 1).astype(BF)
    for b in bs:
        h = b.shape[1] // 2
        keep[:, at : at + h] = dot(pick, b[:, :h], 1, 0)
        send[:, at : at + h] = dot(pick, b[:, h:], 1, 0).astype(BF)
        at += h


def attend_layer_body(layer):
    def body(q, k, v, ko, vo, hid, gains, biases, am, ao, probs, mixed, n1, r1, ln, y):
        attend(q, k, v, ko, vo, probs, mixed)
        y[...] = attend_out(hid, mixed, am, ao, gains[layer, 0:1], biases[layer, 0:1], n1, r1, ln)

    return body


def ffn_part_body(ln, wi, wu, act, dgelu, out):
    out[...] = ffn_half(ln[...], 0, wi, wu, act, dgelu).astype(out.dtype)


def ffn_end_body(y, part, got, gains, biases, am, ao, n2, r2, hid, low, k, v):
    n, r = normalize(y[...] + part[...] + got[...].astype(F32))
    n2[...] = n
    r2[...] = r
    x = n * gains[0, 1:2] + biases[0, 1:2]
    hid[...] = x
    low[...] = x.astype(BF)
    kv_body(low, am, ao, k, v)


def turn_body(y, part, got, gains, biases, grad, hid, mid, lmid, la, lb, vec):
    n, r = normalize(y[...] + part[...] + got[...].astype(F32))
    hid[...] = n * gains[1, 1:2] + biases[1, 1:2]
    middle_back(grad[...], n, r, gains[1, 1:2], mid, lmid, (la, lb), vec)


def rows_joined(pieces):
    return jnp.concatenate([p[...] for p in pieces], axis=0)


def store_rows(x, pieces):
    n = pieces[0].shape[0]
    for i, p in enumerate(pieces):
        p[...] = x[i * n : (i + 1) * n].astype(p.dtype)


def middle_back(grad, n, r, gain, mid, lmid, pieces, vec):
    back, gg, gb = norm_back(grad, n, r, gain)
    mid[...] = back
    lmid[...] = back.astype(BF)
    store_rows(back, pieces)
    vec[0:1] = gg
    vec[1:2] = gb


def ffn_back_own_body(lmid, dgelu, wi, wu, inner, out):
    g = (dot(lmid[...], wu[...], 1, 0) * dgelu[...].astype(F32)).astype(BF)
    inner[...] = g
    out[...] = dot(g, wi[...], 1, 1)


def ffn_back_other_body(la, lb, dgelu, wi, wu, inner, oa, ob):
    g = (dot(rows_joined((la, lb)), wu[...], 1, 0) * dgelu[...].astype(F32)).astype(BF)
    inner[...] = g
    store_rows(dot(g, wi[...], 1, 1), (oa, ob))


def weight_feed_body(sel, lmid, la, lb, ln, lno, act, acto, inner, innero, rest, send):
    n, f = rest.shape[0], act.shape[1]
    for i, (a, ao, b, bo) in enumerate(((lmid[...], rows_joined((la, lb)), act, acto), (ln[...], lno[...], inner, innero))):
        pick = dot(sel[...], a, 1, 1).astype(BF)
        picko = dot(sel[...], ao, 1, 1).astype(BF)
        g = dot(pick, b[...], 1, 0) + dot(picko, bo[...], 1, 0)
        rest[:, i * f : (i + 1) * f] = g[0:n]
        send[:, i * f : (i + 1) * f] = g[n:].astype(BF)


def ffn_back_end_body(layer):
    def body(mid, part, ga, gb, gains, n1, r1, am, ao, res, lres, mix, vec):
        total = mid[...] + part[...] + rows_joined((ga, gb)).astype(F32)
        back, gain_sum, bias_sum = norm_back(total, n1[...], r1[...], gains[layer, 0:1])
        res[...] = back
        low = back.astype(BF)
        lres[...] = low
        vec[0:1] = gain_sum
        vec[1:2] = bias_sum
        h = mix.shape[1] // 2
        for i, w in enumerate(sides(am, ao, OUT)):
            mix[:, i * h : (i + 1) * h] = dot(low, w[...], 1, 0).astype(BF)

    return body


def grad_one_body(sel, a, b, keep, send):
    weight_grad(sel, a, (b,), keep, send)


def grad_two_body(sel, a, b, c, d, keep, send):
    weight_grad(sel, a, (b,), keep, send)
    weight_grad(sel, c, (d,), keep, send, b.shape[1] // 2)


def attend_back_body(mix, mixed, probs, q, v, vo, dscores, *theirs):
    t, width = q.shape
    pairs = width // LANES
    lo, top = halves_of_pair()
    for g in range(pairs):
        sl = slice(g * LANES, (g + 1) * LANES)
        gg = mix[:, sl]
        vv = rows_of(v, vo, g)
        delta = (gg.astype(F32) * mixed[:, sl].astype(F32)).T
        ds = []
        for j, m in enumerate((lo, ~lo)):
            dl = jnp.sum(delta[j * HD : (j + 1) * HD], axis=0, keepdims=True)
            dp = dot(vv, jnp.where(m, gg, 0), 1, 1)
            ds.append((probs[2 * g + j].astype(F32) * (dp - dl)).astype(BF))
            dscores[2 * g + j] = ds[j]
        qq = q[:, sl]
        at = (g + pairs // 2) % pairs * LANES
        count = len(theirs) // 2
        dk, dv = theirs[at * count // width], theirs[count + at * count // width]
        at = at % (width // count)
        to = slice(at, at + LANES)
        dk[:, to] = jnp.where(lo, dot(ds[0][t:], qq, 1, 0), dot(ds[1][t:], qq, 1, 0)).astype(BF)
        dv[:, to] = jnp.where(lo, dot(probs[2 * g, t:], gg, 1, 0), dot(probs[2 * g + 1, t:], gg, 1, 0)).astype(BF)


def attend_back_own(mix, probs, dscores, q, k, ko, res, am, ao, dk, dv, gq, rest):
    t, width = q.shape
    pairs = width // LANES
    lo, top = halves_of_pair()
    for g in range(pairs):
        sl = slice(g * LANES, (g + 1) * LANES)
        gg, qq = mix[:, sl], q[:, sl]
        kk = rows_of(k, ko, g)
        dq = jnp.where(top, dot(kk, dscores[2 * g], 0, 0), dot(kk, dscores[2 * g + 1], 0, 0))
        gq[:, sl] = (dq * SCALE).T.astype(BF)
        dk[:, sl] = jnp.where(lo, dot(dscores[2 * g, :t], qq, 1, 0), dot(dscores[2 * g + 1, :t], qq, 1, 0))
        dv[:, sl] = jnp.where(lo, dot(probs[2 * g, :t], gg, 1, 0), dot(probs[2 * g + 1, :t], gg, 1, 0))
    h = width // 2
    total = res[...]
    for i, w in enumerate(sides(am, ao, QUERY)):
        total = total + dot(gq[:, i * h : (i + 1) * h], w[...], 1, 1)
    rest[...] = total


def hidden_back(rest, dk, dv, ka, kb, va, vb, am, ao, gk, gv):
    total = rest[...]
    for own, theirs, out, n in ((dk, (ka, kb), gk, KEY), (dv, (va, vb), gv, VALUE)):
        h = out.shape[1] // 2
        for i, w in enumerate(sides(am, ao, n)):
            sl = slice(i * h, (i + 1) * h)
            g = (own[:, sl] + theirs[i][...].astype(F32)).astype(BF)
            out[:, sl] = g
            total = total + dot(g, w[...], 1, 1)
    return total


def next_layer_body(rest, dk, dv, ka, kb, va, vb, am, ao, n2, r2, gains, gk, gv, mid, lmid, la, lb, vec):
    grad = hidden_back(rest, dk, dv, ka, kb, va, vb, am, ao, gk, gv)
    middle_back(grad, n2[...], r2[...], gains[0, 1:2], mid, lmid, (la, lb), vec)


def grad_attention_body(sel, lres, mixed, low, gq, gk, gv, keep, send, keep2, send2):
    weight_grad(sel, lres, (mixed,), keep, send)
    weight_grad(sel, low, (gq,), keep, send, mixed.shape[1] // 2)
    weight_grad(sel, low, (gk, gv), keep2, send2)


def split_dot(onehot, x, ca, cb):
    total = None
    for _ in range(3):
        part = x.astype(BF)
        x = x - part.astype(F32)
        y = dot(onehot, part, ca, cb)
        total = y if total is None else total + y
    return total


def last_body(rest, dk, dv, dk2, dv2, am, ao, sel, low, marks, v1, v2, v3, v4, grad_in, keep, send, gk, gv):
    w = gk.shape[1]
    own, h = grad_in.shape[0], w // 2
    grad = hidden_back(rest, dk, dv, dk2[:, :h], dk2[:, h:], dv2[:, :h], dv2[:, h:], am, ao, gk, gv)
    weight_grad(sel, low, (gk, gv), keep, send)
    grad_in[...] = jnp.where(marks[0:own, 0:1] > 0.5, 0.0, grad[0:own])
    mask = jnp.sum(grad * marks[:, 0:1], axis=0, keepdims=True)
    rows = jnp.concatenate([v1[...], v2[...], v3[...], v4[...], jnp.broadcast_to(mask, (8,) + mask.shape[1:])], axis=0)
    rows = jnp.concatenate([rows, jnp.zeros((LANES - rows.shape[0], rows.shape[1]), F32)], axis=0)
    small = split_dot(sel[...], rows, 1, 1)
    keep[:, w:] = small
    send[:, w:] = small.astype(BF)


def join_body(parts):
    def body(*refs):
        keeps, gots, rest, sends = refs[:parts], refs[parts : 2 * parts], refs[2 * parts], refs[2 * parts + 1 :]
        n, at = rest.shape[0], 0
        for keep, got in zip(keeps, gots):
            to = slice(at, at + keep.shape[1])
            rest[:, to] = keep[0:n] + got[0:n].astype(F32)
            for i, x in enumerate(sends):
                sl = slice((i + 1) * n, (i + 2) * n)
                x[:, to] = (keep[sl] + got[sl].astype(F32)).astype(BF)
            at += keep.shape[1]

    return body


def add_body(keep, got, rest, send):
    n = rest.shape[0]
    rest[...] = keep[0:n] + got[0:n].astype(F32)
    send[...] = (keep[n:] + got[n:].astype(F32)).astype(BF)


def top_body(*refs):
    n = len(refs) - 2
    parts, (grad, marks) = refs[:n], refs[n:]
    h = grad.shape[0] // n
    lane = lax.broadcasted_iota(I32, (1, LANES), 1)
    edges = jnp.full((1, LANES), -8.0, F32)
    bounds = []
    for j, p in enumerate(parts):
        tail = p[2 * h :].astype(F32)
        b = tail.shape[0] - 8
        edges = jnp.where((lane >= j * b) & (lane < (j + 1) * b), edges_of(tail), edges)
        bounds.append(tail[0:b])
    bounds = jnp.concatenate(bounds, axis=0)
    bounds = jnp.concatenate([bounds, jnp.zeros((LANES - bounds.shape[0], bounds.shape[1]), F32)], axis=0).astype(BF)
    row = lax.broadcasted_iota(I32, (h, 1), 0)
    even = (lane % 2) == 0
    for j, p in enumerate(parts):
        pos = (row + block_place(j, h)).astype(F32)
        onehot = jnp.where(pos == edges, 1.0, 0.0).astype(BF)
        grad[j * h : (j + 1) * h] = p[h : 2 * h].astype(F32) + dot(onehot, bounds, 1, 0)
        after = jnp.where((even & (pos > edges)) & (edges > -4.0), 1.0, 0.0) - jnp.where((~even & (pos >= edges)) & (edges > -4.0), 1.0, 0.0)
        marks[j * h : (j + 1) * h] = jnp.broadcast_to(jnp.sum(after, axis=1, keepdims=True), (h, LANES))


def block_place(j, own):
    return (lax.axis_index("seq") ^ j) * (2 * own) + lax.axis_index("mp") * own


def edges_of(payload):
    e = payload[-8:, 0:LANES].astype(F32)
    return e[0:1] * 16.0 + e[4:5]


def result_body(hid, payload, out):
    own = hid.shape[0] // lax.axis_size("seq")
    n = out.shape[0] - own
    out[0:own] = hid[0:own]
    row = jnp.broadcast_to(edges_of(payload), (8, LANES)).T[0:n, 0:1]
    lane = lax.broadcasted_iota(I32, (1, own), 1)
    total = None
    for j in range(hid.shape[0] // own):
        pos = (lane + block_place(j, own)).astype(F32)
        onehot = jnp.where(row == pos, 1.0, 0.0).astype(BF)
        y = split_dot(onehot, hid[j * own : (j + 1) * own], 1, 0)
        total = y if total is None else total + y
    out[own:] = total


def put_body(mine, other, out, bound, rows, sems):
    n = bound.shape[1] * 2
    own = mine.shape[0] - n
    m = lax.axis_index("mp")
    a = pltpu.make_async_copy(mine.at[0:own], out.at[0, pl.ds(m * own, own)], sems.at[0])
    b = pltpu.make_async_copy(other.at[0:own], out.at[0, pl.ds((1 - m) * own, own)], sems.at[1])
    a.start()
    b.start()
    total = mine[own:] + other[own:]
    for i in range(n // 2):
        rows[i] = total[2 * i : 2 * i + 2]
    c = pltpu.make_async_copy(rows, bound.at[0], sems.at[2])
    c.start()
    a.wait()
    b.wait()
    c.wait()


def place_body(mine, other, out, sems):
    own = mine.shape[0]
    m = lax.axis_index("mp")
    a = pltpu.make_async_copy(mine, out.at[0, pl.ds(m * own, own)], sems.at[0])
    b = pltpu.make_async_copy(other, out.at[0, pl.ds((1 - m) * own, own)], sems.at[1])
    a.start()
    b.start()
    a.wait()
    b.wait()


def finish_body(places, width, terms):
    def body(*refs):
        layers, outs = (refs[: terms[0]], refs[terms[0] : sum(terms)]), refs[sum(terms) :]

        def total(i, sl):
            x = layers[i][0][:, sl]
            for r in layers[i][1:]:
                x = x + r[:, sl].astype(F32)
            return x

        for i in range(LAYERS):
            for j, at in enumerate(places):
                outs[j][i] = total(i, slice(at[i], at[i] + width))
        if len(outs) > len(places):
            gain, bias, mask = outs[len(places) :]
            small = total(0, slice(4 * width, 4 * width + LANES)).T
            for i in range(LAYERS):
                for j in range(2):
                    at = 4 * i + 2 * j
                    gain[i, j : j + 1] = small[at : at + 1]
                    bias[i, j : j + 1] = small[at + 1 : at + 2]
            mask[...] = small[8:9]

    return body


def order_of(masks):
    if not masks:
        return [0]
    rest = order_of(masks[1:])
    return rest + [r ^ masks[0] for r in rest]


def tie(x, *others):
    return lax.optimization_barrier((x,) + others)[0]


def on_device(inputs, span_info, mask_vector, w_query, w_key, w_value, w_output, w_inner, w_outer, norm_gain, norm_bias, grad_output, grad_bounds):
    t, d = inputs.shape[1:]
    ns, nd = lax.axis_size("seq"), lax.axis_size("dp")
    s, z = lax.axis_index("seq"), lax.axis_index("dp")
    f = w_inner.shape[2]
    hw = w_query.shape[2]
    heads = 2 * hw // HD
    own = t // 2
    tok = own * ns
    axes = ("dp", "seq")
    masks = []
    bit = ns
    while bit < ns * nd:
        masks.append(bit)
        bit *= 2
    here = z * ns + s
    dma = lambda n: pltpu.SemaphoreType.DMA((n,))
    buf = lambda *dims: pltpu.VMEM(dims, BF)

    def to_role(x):
        return x

    def gather(x):
        return [x] + [flip(x, axes, j) for j in range(1, ns)]

    spans = span_info.shape[1]
    def other(*xs):
        return [flip(x, "mp", 1) for x in xs]

    weights = (w_key, w_value, w_query, w_output)
    attention = shape((4, d, hw), BF)
    packet, am0 = run(
        start_body, (shape((2 * own + 2 * spans + 8, d), BF), attention),
        span_info, mask_vector, inputs, grad_output, grad_bounds, *weights, name="start", smem=1, hbm=8,
        scratch=(pltpu.VMEM((own, d), F32), pltpu.VMEM((1, d), F32), pltpu.VMEM((own, d), F32), pltpu.VMEM((spans, 2, d), F32),
                 dma(4), dma(4)),
    )
    held0 = other(am0)[0]
    packets = gather(packet)
    feed_weight = shape((d, f), BF)
    am1, wi0, wu0, wi1, wu1 = run(
        load_body, (attention,) + (feed_weight,) * 4, *weights, w_inner, w_outer, name="load", hbm=6, scratch=(dma(8),), after=(packet,)
    )

    per = d // (ns * nd)
    base = jnp.concatenate([(here ^ r) * per + jnp.arange(per, dtype=I32) for r in order_of(masks)])
    sel = (base[:, None] == jnp.arange(d, dtype=I32)[None, :]).astype(BF)
    picks = sel.shape[0]
    gains, biases = norm_gain.transpose(0, 2, 1), norm_bias.transpose(0, 2, 1)

    full = shape((tok, d))
    full_low = shape((tok, d), BF)
    column = shape((tok, 1))
    wide = shape((tok, 2 * f), BF)
    kv_shape = shape((tok, 4 * hw), BF)
    prob_shape = shape((heads, 2 * tok, tok), BF)
    piece = (shape((picks, f)), shape((picks, f), BF))
    two = shape((2, d))

    hid, low, k, v, ao0 = run(
        kv_first_body, (full, full_low, full_low, full_low, attention), *packets, am0, held0,
        name="keys_first", hbm=1, scratch=(dma(4),), after=(sel, am1),
    )
    ko, vo = other(k, v)
    (q,) = run(q_body, (full_low,), low, am0, ao0, name="queries")
    ao1 = other(tie(am1, ko, vo))[0]
    narrow = shape((tok, f), BF)

    def attend_layer(layer, q, k, v, ko, vo, hid, am, ao):
        return run(
            attend_layer_body(layer), (prob_shape, full_low, full, column, full_low, full),
            q, k, v, ko, vo, hid, gains, biases, am, ao, name="attend", limit=BIG,
        )

    def ffn(ln, wi, wu):
        lno = other(ln)[0]
        act, dgelu, part = run(ffn_part_body, (narrow, narrow, full), ln, wi, wu, name="ffn_own")
        acto, dgeluo, parto = run(ffn_part_body, (narrow, narrow, full_low), lno, wi, wu, name="ffn_other", after=(part,))
        return lno, act, dgelu, acto, dgeluo, part, other(parto)[0]

    probs, mixed, n1, r1, ln, y = attend_layer(0, q, k, v, ko, vo, hid, am0, ao0)
    lno, act, dgelu, acto, dgeluo, part, got = ffn(ln, wi0, wu0)
    n2, r2, hid, low1, k1, v1 = run(
        ffn_end_body, (full, column, full, full_low, full_low, full_low), y, part, got, gains, biases, am1, ao1, name="ffn_end"
    )
    k1o, v1o = other(k1, v1)
    grad, marks = run(top_body, (full, shape((tok, LANES))), *packets, name="top", after=(k1,))
    (q1,) = run(q_body, (full_low,), low1, am1, ao1, name="queries", after=(grad,))
    probs1, mixed1, n11, r11, ln1, y = attend_layer(1, q1, k1, v1, k1o, v1o, hid, am1, ao1)
    ln1o, act1, dgelu1, act1o, dgelu1o, part, got = ffn(ln1, wi1, wu1)
    halved = (shape((tok // 2, d), BF),) * 2
    hid, mid, lmid, la, lb, vec2 = run(turn_body, (full, full, full_low) + halved + (two,), y, part, got, gains, biases, grad, name="turn")

    def join(pairs, blocks=2, after=()):
        width = sum(k.shape[1] for k, _ in pairs)
        n = picks // blocks
        return run(
            join_body(len(pairs)), (shape((n, width)),) + (shape((n, width), BF),) * (blocks - 1),
            *[k for k, _ in pairs], *[g for _, g in pairs], name="join", after=after,
        )

    def spread(pairs, after=()):
        if nd > 4:
            pair = send_on(join(pairs, after=after), 0)
            for i in range(1, len(masks)):
                pair = send_on(add(pair), i)
            return pair
        keep, *sends = join(pairs, nd, after=after)
        return [keep] + [flip(x, axes, o) for x, o in zip(sends, order_of(masks)[1:])]

    def send_on(pair, step):
        return pair[0], flip(pair[1], axes, masks[step])

    def add(pair, after=(), us=1.0):
        keep, got = pair
        n, w = keep.shape[0] // 2, keep.shape[1]
        if n % 16:
            total = keep + got.astype(F32)
            return total[:n], total[n:].astype(BF)
        return run(add_body, (shape((n, w)), shape((n, w), BF)), keep, got, name="add", after=after, us=us)

    def rest(pair):
        for i in range(2, len(masks)):
            pair = send_on(add(pair), i)
        return pair

    def halves(keep, send):
        return keep, flip(send, "mp", 1)

    group = (shape((picks // 2, 2 * f)), shape((picks // 2, 2 * f), BF))

    def ffn_back(layer, mid, lmid, lmids, dgelu, dgeluo, wi, wu, n1, r1, am, ao, after=(), between=None):
        lmids = other(*lmids)
        inner, part = run(ffn_back_own_body, (narrow, full), lmid, dgelu, wi, wu, name="ffn_back_own", after=after)
        innero, *parts = run(
            ffn_back_other_body, (narrow,) + halved, *lmids, dgeluo, wi, wu, name="ffn_back_other", after=(part,)
        )
        gots = other(*parts)
        ends = run(
            ffn_back_end_body(layer), (full, full_low, full_low, two), mid, part, *gots, gains, n1, r1, am, ao,
            name="ffn_back_end", after=between(lmids, inner, innero),
        )
        return (lmids, inner, innero) + tuple(ends)

    def grad_feed(lmid, lmids, ln, lno, act, acto, inner, innero, after=()):
        return run(weight_feed_body, group, sel, lmid, *lmids, ln, lno, act, acto, inner, innero, name="grad_feed", after=after)

    def attend_own(mix, probs, dscores, q, k, ko, res, am, ao, after=()):
        return run(
            attend_back_own, (full, full, full_low, full), mix, probs, dscores, q, k, ko, res, am, ao,
            name="attend_back_own", after=after,
        )

    def attend_back(mix, mixed, probs, q, v, vo, after=()):
        return run(
            attend_back_body, (prob_shape, shape((tok, 4 * hw), BF)), mix, mixed, probs, q, v, vo, name="attend_back", us=2.3, after=after
        )

    def grad_pair(a, b, after=(), name=None, us=0.9):
        w = b.shape[1] // 2
        return run(grad_one_body, (shape((picks, w)), shape((picks, w), BF)), sel, a, b, name=name, us=us, after=after)

    sums = {}

    def between(lmids, inner, innero):
        sums["ffn"] = grad_feed(lmid, lmids, ln1, ln1o, act1, act1o, inner, innero)
        return (sums["ffn"][0],)

    _, _, _, res, lres1, mix, vec1 = ffn_back(
        1, mid, lmid, (la, lb), dgelu1, dgelu1o, wi1, wu1, n11, r11, am1, ao1, between=between
    )
    ffn1 = send_on(sums["ffn"], 0)
    theirs = (shape((tok, hw), BF),) * 4
    dscores, *dkv2 = run(attend_back_body, (prob_shape,) + theirs, mix, mixed1, probs1, q1, v1, v1o, name="attend_back")
    dkv2 = other(*dkv2)
    dk, dv, gq, part_sum = attend_own(mix, probs1, dscores, q1, k1, k1o, res, am1, ao1)
    gk, gv, mid, lmid, la, lb, vec02 = run(
        next_layer_body, (full_low, full_low, full, full_low) + halved + (two,), part_sum, dk, dv, *dkv2, am1, ao1, n2, r2, gains, name="next_layer"
    )
    attn = (shape((picks, 2 * hw)), shape((picks, 2 * hw), BF))
    keep, send, keep2, send2 = run(
        grad_attention_body, attn * 2, sel, lres1, mixed1, low1, gq, gk, gv, name="grad_attention", after=(mid,)
    )
    att1 = halves(keep, send), halves(keep2, send2)
    def between(lmids, inner, innero):
        sums["ffn"] = add(ffn1, after=(innero,))
        sums["attention"] = join(att1, after=(sums["ffn"][0],))
        return (sums["attention"][0],)

    lmids, inner, innero, res, lres0, mix, vec01 = ffn_back(
        0, mid, lmid, (la, lb), dgelu, dgeluo, wi0, wu0, n1, r1, am0, ao0, after=(keep,), between=between
    )
    att1 = send_on(sums["attention"], 0)
    dscores, *dkv2 = run(attend_back_body, (prob_shape, full_low, full_low), mix, mixed, probs, q, v, vo, name="attend_back")
    dkv2 = other(*dkv2)
    ffn0 = grad_feed(lmid, lmids, ln, lno, act, acto, inner, innero, after=(dscores,))
    ffn0 = send_on(ffn0, 0)
    dk, dv, gq, part_sum = attend_own(mix, probs, dscores, q, k, ko, res, am0, ao0, after=(ffn0[0],))
    (keep, got), (first, first_send) = att1, sums["ffn"]
    n, w = first.shape[0], first.shape[1] + keep.shape[1]
    layer1 = run(
        add_beside_body, (shape((n, w)), shape((n, w), BF)), keep, got, first, first_send, name="add_beside", us=LONG, after=(dk,)
    )
    (res_out,) = run(result_body, (shape((own + 2 * spans, d)),), hid, packets[0], name="result", after=(layer1[0],))
    layer1 = send_on(layer1, 1)
    query0 = halves(*run(
        grad_two_body, (shape((picks, 2 * hw)), shape((picks, 2 * hw), BF)), sel, lres0, mixed, low, gq, name="grad_query", after=(res_out,)
    ))
    attn = (shape((picks, 2 * hw + LANES)), shape((picks, 2 * hw + LANES), BF))
    grad_in, keep, send = run(
        last_body, (shape((own, d)),) + attn, part_sum, dk, dv, *dkv2, am0, ao0, sel, low, marks, vec01, vec02, vec1, vec2,
        name="last", scratch=(buf(tok, 2 * hw), buf(tok, 2 * hw)), after=(query0[0],),
    )
    key0 = halves(keep, send)
    att0 = join([query0, key0], after=(grad_in,))
    ffn0 = add(ffn0, after=(att0[0], layer1[1]), us=COST)
    att0 = send_on(att0, 0)
    ffn0 = send_on(ffn0, 1)
    att0 = send_on(add(att0, after=(ffn0[0],)), 1)
    layer1, ffn0, att0 = [rest(x) for x in (layer1, ffn0, att0)]
    (grad_inputs,) = run(
        place_body, (shape((1, t, d)),), grad_in, flip(grad_in, "mp", 1), name="grad_inputs", scratch=(dma(2),), out_specs=(HB,)
    )
    res_out = to_role(res_out)
    outputs, bound_rows = run(
        put_body, (shape((1, t, d)), shape((1, spans, 2, d))), res_out, flip(res_out, "mp", 1),
        name="put", scratch=(pltpu.VMEM((spans, 2, d), F32), dma(3)), out_specs=(HB, HB),
    )

    def finish(layers, places, width, extra=(), name=None):
        outs = (shape((LAYERS, per, width)),) * len(places) + tuple(extra)
        return pl.pallas_call(
            finish_body(places, width, [len(x) for x in layers]), out_shape=outs,
            compiler_params=pltpu.CompilerParams(vmem_limit_bytes=LIMIT), name=name,
        )(*layers[0], *layers[1])

    g_outer, g_inner = finish((ffn0, layer1), [(0, 0), (f, f)], f, name="finish_feed")
    vec_shape = shape((LAYERS, 2, per))
    at = 2 * hw
    g_output, g_query, g_key, g_value, g_gain, g_bias, g_mask = finish(
        (att0, layer1), [(0, 2 * f), (hw, 2 * f + hw), (at, 2 * f + at), (at + hw, 2 * f + at + hw)], hw,
        (vec_shape, vec_shape, shape((1, per))), name="finish_attention",
    )
    return outputs, bound_rows, grad_inputs, g_mask, g_query, g_key, g_value, g_output, g_inner, g_outer, g_gain.transpose(0, 2, 1), g_bias.transpose(0, 2, 1)


def solution(mesh):
    row = P("dp", "seq", None)
    wide = P(None, None, "mp")
    out_w = P(None, ("dp", "seq"), "mp")
    out_v = P(None, ("dp", "seq"), None)
    return jax.shard_map(
        on_device,
        mesh=mesh,
        in_specs=(row, row, P(), wide, wide, wide, wide, wide, wide, P(), P(), row, P("dp", "seq", None, None)),
        out_specs=(row, P("dp", "seq", None, None), row, P(None, ("dp", "seq"))) + (out_w,) * 6 + (out_v,) * 2,
        check_vma=False,
    )
```
